128 devices in a mesh: dp: 16 (over z, y_lo, core), tensor: 8 (over x, y_hi).
Axes of the slice: x: 4, y: 4 (y_hi: 2, y_lo: 2; y = y_hi * 2 + y_lo), z: 4, core: 2. Of those that a mesh axis runs over, the one named last changes fastest.
Arguments:
- text_rows: bfloat16 [28672, 8192], P('dp', 'tensor'), may hold values from -6 to 6
- vis_rows: bfloat16 [24576, 8192], P('dp', 'tensor'), may hold values from -6 to 6
- q_weight: bfloat16 [8192, 4096], P('dp', 'tensor'), may hold values from -40 to 40
- kv_weight: bfloat16 [8192, 2, 1024], P(None, None, 'tensor'), may hold values from -40 to 40
- q_bias: float32 [4096], P('tensor'), may hold values from -3 to 3
- kv_bias: float32 [2, 1024], P(None, 'tensor'), may hold values from -3 to 3
- norm_gain: float32 [8192], replicated, may hold values from 0.1 to 1.9
- tile_dest: int32 [16, 6], replicated, may hold values from 0 to 15, as said below
- tile_block: int32 [16, 6], P('dp'), may hold values from 0 to 6, as said below
- doc_lens: int32 [16, 4], P('dp'), may hold values from 1 to 896, 1792 in all within a row
Outputs:
- context: bfloat16 [28672, 4096], P('dp', 'tensor')
The draws below stay inside these ranges and needn't reach their ends.
Inputs may be any that keep to these rules, and one draw needn't show every extreme that they name: `tile_dest`: each column j names every sequence once, and the 6 tiles of one vision shard go to different sequences. `tile_block`: the 6 blocks of one sequence are different.
All inputs are finite; a program needn't handle non-finite values.
Results may differ from the reference program's by a relative error of at most 0.0048.
Values may be sent and summed in bfloat16 or wider, within the bound.
No kernel may reach another device: no remote copies, remote signals or barrier semaphores. Data moves between devices by JAX's collectives and lax.ppermute only.
A program may use at most 256 MiB of HBM per device.

```python
import math
import jax
import jax.numpy as jnp
import numpy as np
from jax import lax

D = 8192
HEADS = 32
KV_HEADS = 8
HD = 128
SEQ = 1792
TILE = 256
TILE_DEV = 6
DOCS = 4
TOKENS = 28672
VIS = 24576
N_DP = 16


def draw_q_weight(key, part):
    key = jax.random.fold_in(key, 11)
    noise_key = jax.random.fold_in(key, 0)
    drawn = jax.random.normal(noise_key, (D, HEADS * HD), jnp.float32) * D ** (-0.5)
    return drawn.astype(jnp.bfloat16)


def draw_kv_weight(key, part):
    key = jax.random.fold_in(key, 23)
    drawn = jax.random.normal(key, (D, 2, KV_HEADS * HD), jnp.float32) * D ** (-0.5)
    return drawn.astype(jnp.bfloat16)


def draw_tile_dest(key, part):
    key = jax.random.fold_in(key, 37)
    label_key, owner_key = jax.random.split(key)
    labels = jax.random.permutation(label_key, N_DP).astype(jnp.int32)
    inverse = jnp.argsort(labels).astype(jnp.int32)
    owners = jax.random.permutation(owner_key, N_DP).astype(jnp.int32)
    columns = []
    for slot_index in range(TILE_DEV):
        moved = inverse[(labels + slot_index) % N_DP]
        columns.append(owners[moved])
    return jnp.stack(columns, axis=1).astype(jnp.int32)


def draw_tile_block(key, part):
    key = jax.random.fold_in(key, 53)
    row_keys = jax.random.split(key, N_DP)
    blocks = jax.vmap(lambda row_key: jax.random.permutation(row_key, SEQ // TILE)[:TILE_DEV])(row_keys)
    return blocks.astype(jnp.int32)


def steps_of(rng, dims, shards, low, top_value):
    def one(axis_at, shards_of):
        heights = jax.random.uniform(jax.random.fold_in(jax.random.fold_in(rng, 6), axis_at), (shards_of,), jnp.float32, low / len(shards), top_value / len(shards))
        return jnp.repeat(jnp.exp(heights), dims[axis_at] // shards_of).reshape((-1,) + (1,) * (len(dims) - axis_at - 1))

    loudness = one(*shards[0])
    for cut in shards[1:]:
        loudness = loudness * one(*cut)
    return loudness


def profile(count, total, limit, lean):
    weights = [(1 << 20) // math.isqrt(grade ** lean) + 1 for grade in range(2, count + 1)]
    rest, given = total - limit - (count - 1), [1] * (count - 1)
    while rest > 0:
        free = [i for i in range(count - 1) if given[i] < limit]
        pool, remaining = sum([weights[i] for i in free]), rest
        for i in free:
            more = min(limit - given[i], max(1, remaining * weights[i] // pool), rest)
            given[i] = given[i] + more
            rest = rest - more
    return np.array([limit] + given)


def uneven_parts(stream_key, count, total, limit, lean):
    if count == 2:
        one = jax.random.randint(stream_key, (), max(1, total - limit), min(limit, total - 1) + 1)
        return jnp.stack([one, total - one])
    tallies = jnp.asarray(profile(count, total, limit, lean), jnp.int32)
    pairs = (count - 1) // 2
    giver, taker = tallies[1:1 + 2 * pairs:2], tallies[2:2 + 2 * pairs:2]
    margin = jnp.minimum(giver - 1, limit - taker)
    passed = jax.random.randint(jax.random.fold_in(stream_key, 1), (pairs,), 0, 1 << 20) % (margin + 1)
    tallies = tallies.at[1:1 + 2 * pairs:2].set(giver - passed).at[2:2 + 2 * pairs:2].set(taker + passed)
    return tallies[jax.random.permutation(jax.random.fold_in(stream_key, 2), count)]


def scatter_about(own_key, extent, scale, most, cuts=(), kind=jnp.bfloat16):
    drawn = scale * jax.random.normal(own_key, extent, jnp.float32)
    if cuts:
        drawn = drawn * steps_of(own_key, extent, cuts, -0.22, 0.18)
    return jnp.clip(drawn, -most, most).astype(kind)


def setup_inputs(seed: int = 0) -> dict:
    key_of = jax.random.split(jax.random.key(seed), 11)
    return {
        "text_rows": scatter_about(key_of[0], (TOKENS, D), 1.0, 6.0, ((0, 16), (1, 8))),
        "vis_rows": scatter_about(key_of[1], (VIS, D), 1.0, 6.0, ((0, 16), (1, 8))),
        "q_weight": draw_q_weight(jax.random.fold_in(key_of[10], 71), 0),
        "kv_weight": draw_kv_weight(jax.random.fold_in(key_of[10], 71), 0),
        "q_bias": scatter_about(key_of[4], (HEADS * HD,), 0.5, 3.0, ((0, 8),), jnp.float32),
        "kv_bias": scatter_about(key_of[5], (2, KV_HEADS * HD), 0.5, 3.0, ((1, 8),), jnp.float32),
        "norm_gain": jnp.clip(1.0 + 0.18 * jax.random.normal(key_of[6], (D,), jnp.float32), 0.1, 1.9),
        "tile_dest": draw_tile_dest(jax.random.fold_in(key_of[10], 71), 0),
        "tile_block": draw_tile_block(jax.random.fold_in(key_of[10], 71), 0),
        "doc_lens": jax.vmap(lambda own: uneven_parts(own, DOCS, SEQ, SEQ // 2, 2))(jax.random.split(key_of[9], N_DP)).reshape((N_DP, DOCS)).astype(jnp.int32),
    }


rope_base = 1000000.0
eps = 1e-06
masked_score = -1e+30

def rope_tables(length, width):
    half_width = width // 2
    inverse = rope_base ** (-(jnp.arange(half_width, dtype=jnp.float32) * 2.0) / width)
    angles = jnp.arange(length, dtype=jnp.float32)[:, None] * inverse[None, :]
    return (jnp.cos(angles), jnp.sin(angles))

def rotate(values, cosine_table, sine_table):
    half_width = values.shape[-1] // 2
    front = values[..., :half_width]
    back = values[..., half_width:]
    cosine = cosine_table[:, None, :]
    sine_part = sine_table[:, None, :]
    return jnp.concatenate([front * cosine - back * sine_part, back * cosine + front * sine_part], axis=-1)

def normalize(rows, gain):
    floats = rows.astype(jnp.float32)
    spread = lax.optimization_barrier(jnp.mean(floats * floats, axis=-1, keepdims=True))
    return (floats * lax.rsqrt(spread + eps) * gain.astype(jnp.float32)).astype(jnp.bfloat16)

def place_tiles(rows, tiles, blocks):
    tile_len = tiles.shape[1]
    for slot_index in range(tiles.shape[0]):
        start_row = (blocks[slot_index] * tile_len).astype(jnp.int32)
        rows = lax.dynamic_update_slice_in_dim(rows, tiles[slot_index], start_row, 0)
    return rows

def document_ids(lens, length):
    ends = jnp.cumsum(lens)
    positions = jnp.arange(length, dtype=jnp.int32)
    return lax.optimization_barrier(jnp.sum((positions[:, None] >= ends[None, :]).astype(jnp.int32), axis=1))

def attend(query_rows, key_rows, value_rows, documents):
    length = query_rows.shape[0]
    score_scale = 1.0 / math.sqrt(query_rows.shape[-1])
    scores = jnp.einsum('qhgd,khd->hgqk', query_rows.astype(jnp.float32), key_rows.astype(jnp.float32)) * score_scale
    positions = jnp.arange(length, dtype=jnp.int32)
    allowed = (documents[:, None] == documents[None, :]) & (positions[None, :] <= positions[:, None])
    scores = jnp.where(allowed[None, None], scores, masked_score)
    row_top = lax.optimization_barrier(jnp.max(scores, axis=-1, keepdims=True))
    weights = jnp.exp(scores - row_top)
    probs = (weights / lax.optimization_barrier(jnp.sum(weights, axis=-1, keepdims=True))).astype(jnp.bfloat16)
    mixed = jnp.einsum('hgqk,khd->qhgd', probs.astype(jnp.float32), value_rows.astype(jnp.float32))
    return mixed.astype(jnp.bfloat16).reshape(length, -1)

def reference(text_rows, vis_rows, q_weight, kv_weight, q_bias, kv_bias, norm_gain, tile_dest, tile_block, doc_lens):
    owner_ids = jnp.arange(N_DP, dtype=jnp.int32)
    sources = lax.optimization_barrier(jnp.sum(jnp.where(tile_dest[None, :, :] == owner_ids[:, None, None], owner_ids[None, :, None], 0), axis=1))
    tiles = vis_rows.reshape(N_DP, TILE_DEV, TILE, D)
    picked = tiles[sources, jnp.arange(TILE_DEV, dtype=jnp.int32)[None, :]]
    cosine_table, sine_table = rope_tables(SEQ, HD)
    kv_flat = kv_weight.reshape(D, 2 * KV_HEADS * HD)

    def one_owner(packed):
        rows, chosen, blocks, lens = packed
        merged = place_tiles(rows, chosen, blocks)
        normed = normalize(merged, norm_gain)
        query_sum = jnp.dot(normed, q_weight, preferred_element_type=jnp.float32) + q_bias
        pair_sum = jnp.dot(normed, kv_flat, preferred_element_type=jnp.float32).reshape(SEQ, 2, KV_HEADS * HD) + kv_bias
        query_rows = rotate(query_sum.reshape(SEQ, HEADS, HD), cosine_table, sine_table).astype(jnp.bfloat16)
        key_rows = rotate(pair_sum[:, 0].reshape(SEQ, KV_HEADS, HD), cosine_table, sine_table).astype(jnp.bfloat16)
        value_rows = pair_sum[:, 1].reshape(SEQ, KV_HEADS, HD).astype(jnp.bfloat16)
        documents = document_ids(lens, SEQ)
        grouped = query_rows.reshape(SEQ, KV_HEADS, HEADS // KV_HEADS, HD)
        return attend(grouped, key_rows, value_rows, documents)
    context = lax.map(one_owner, (text_rows.reshape(N_DP, SEQ, D), picked, tile_block, doc_lens))
    return context.reshape(N_DP * SEQ, HEADS * HD)
```

```python
import math

import jax
import jax.numpy as jnp
from jax import lax
from jax.experimental import pallas as pl
from jax.experimental.pallas import tpu as pltpu
from jax.sharding import PartitionSpec as P

HD = 128
TILE = 256
BLOCKS = 7
SEQ = BLOCKS * TILE
HALF = SEQ // 2
PART = 1024
SLICE = 2 * PART
WIDE = 2 * HD
QUARTER = HALF // 2
VMEM = 48 * 1024 * 1024

rope_base = 1000000.0
eps = 1e-06
masked_score = -1e30


def params():
    return pltpu.CompilerParams(vmem_limit_bytes=VMEM)


def cost(flops, moved, transcendentals=0):
    return pl.CostEstimate(flops=flops, bytes_accessed=moved, transcendentals=transcendentals)


def rope_tables(length, width):
    half_width = width // 2
    inverse = rope_base ** (-(jnp.arange(half_width, dtype=jnp.float32) * 2.0) / width)
    angles = jnp.arange(length, dtype=jnp.float32)[:, None] * inverse[None, :]
    cosine, sine = jnp.cos(angles), jnp.sin(angles)
    return (
        jnp.concatenate([cosine, cosine], axis=1),
        jnp.concatenate([-sine, sine], axis=1),
    )


def shift_x(value, step):
    pairs = [
        (2 * x + high, 2 * ((x + step) % 4) + high) for x in range(4) for high in range(2)
    ]
    return lax.ppermute(value, "tensor", pairs)


def swap_high(value):
    return lax.ppermute(value, "tensor", [(t, t ^ 1) for t in range(8)])


def transpose_weight(value):
    pairs = []
    for z in range(4):
        for low in range(2):
            for core in range(2):
                for x in range(4):
                    for high in range(2):
                        source = ((z * 2 + low) * 2 + core) * 8 + x * 2 + high
                        there = (((x - z) % 4 * 2 + (low ^ high)) * 2 + core) * 8 + z * 2 + high
                        pairs.append((source, there))
    return lax.ppermute(value, ("dp", "tensor"), pairs)


def norm_kernel(picks, tiles, text, scale, gain, out):
    step = pl.program_id(0)

    def put(rows):
        out[...] = (rows[...].astype(jnp.float32) * scale[...] * gain[...]).astype(jnp.bfloat16)

    @pl.when(step < BLOCKS - 1)
    def _():
        put(tiles)

    @pl.when(step == BLOCKS - 1)
    def _():
        put(text)


def norm_rows(pick, tiles, text, scale, gain):
    grid_spec = pltpu.PrefetchScalarGridSpec(
        num_scalar_prefetch=1,
        grid=(BLOCKS,),
        in_specs=[
            pl.BlockSpec((TILE, PART), lambda i, s: (jnp.minimum(i, BLOCKS - 2), 0)),
            pl.BlockSpec((TILE, PART), lambda i, s: (s[0], 0)),
            pl.BlockSpec((TILE, 1), lambda i, s: (i, 0)),
            pl.BlockSpec((1, PART), lambda i, s: (0, 0)),
        ],
        out_specs=pl.BlockSpec((TILE, PART), lambda i, s: (i, 0)),
    )
    return pl.pallas_call(
        norm_kernel,
        grid_spec=grid_spec,
        out_shape=jax.ShapeDtypeStruct((SEQ, PART), jnp.bfloat16),
        compiler_params=params(),
        cost_estimate=cost(3 * SEQ * PART, 4 * SEQ * PART),
        name="norm_rows",
    )(pick, tiles, text, scale, gain)


def product(own, other, weight):
    both = jnp.dot(own[...], weight[0, :PART], preferred_element_type=jnp.float32)
    return both + jnp.dot(other[...], weight[0, PART:], preferred_element_type=jnp.float32)


def far_kernel(own, other, weight, first, second):
    step = pl.program_id(0)
    result = product(own, other, weight).astype(jnp.bfloat16)

    @pl.when(step < 2)
    def _():
        first[...] = result

    @pl.when(step >= 2)
    def _():
        second[...] = result


def far_parts(own, other, weight, place):
    half = jax.ShapeDtypeStruct((HALF, WIDE), jnp.bfloat16)
    return pl.pallas_call(
        far_kernel,
        grid=(4,),
        in_specs=[
            pl.BlockSpec((QUARTER, PART), lambda i: (i, 0)),
            pl.BlockSpec((QUARTER, PART), lambda i: (i, 0)),
            pl.BlockSpec((1, SLICE, WIDE), lambda i: place),
        ],
        out_specs=[
            pl.BlockSpec((QUARTER, WIDE), lambda i: (jnp.minimum(i, 1), 0)),
            pl.BlockSpec((QUARTER, WIDE), lambda i: (jnp.maximum(i - 2, 0), 0)),
        ],
        out_shape=[half, half],
        compiler_params=params(),
        cost_estimate=cost(2 * SEQ * SLICE * WIDE, 2 * SEQ * SLICE),
        name="far_parts",
    )(own, other, weight)


def near_kernel(own, other, weight_up, weight_down, got_up, got_down, up, down):
    step = pl.program_id(0)
    upward = product(own, other, weight_up)
    downward = product(own, other, weight_down)

    @pl.when(step < 2)
    def _():
        up[...] = (upward + got_up[...].astype(jnp.float32)).astype(jnp.bfloat16)
        down[...] = downward.astype(jnp.bfloat16)

    @pl.when(step >= 2)
    def _():
        up[...] = upward.astype(jnp.bfloat16)
        down[...] = (downward + got_down[...].astype(jnp.float32)).astype(jnp.bfloat16)


def near_parts(own, other, weight_up, place_up, weight_down, place_down, got_up, got_down):
    whole = jax.ShapeDtypeStruct((SEQ, WIDE), jnp.bfloat16)
    return pl.pallas_call(
        near_kernel,
        grid=(4,),
        in_specs=[
            pl.BlockSpec((QUARTER, PART), lambda i: (i, 0)),
            pl.BlockSpec((QUARTER, PART), lambda i: (i, 0)),
            pl.BlockSpec((1, SLICE, WIDE), lambda i: place_up),
            pl.BlockSpec((1, SLICE, WIDE), lambda i: place_down),
            pl.BlockSpec((QUARTER, WIDE), lambda i: (jnp.minimum(i, 1), 0)),
            pl.BlockSpec((QUARTER, WIDE), lambda i: (jnp.maximum(i - 2, 0), 0)),
        ],
        out_specs=[
            pl.BlockSpec((QUARTER, WIDE), lambda i: (i, 0)),
            pl.BlockSpec((QUARTER, WIDE), lambda i: (i, 0)),
        ],
        out_shape=[whole, whole],
        compiler_params=params(),
        cost_estimate=cost(4 * SEQ * SLICE * WIDE, 2 * SEQ * SLICE),
        name="near_parts",
    )(own, other, weight_up, weight_down, got_up, got_down)


def finish_kernel(
    rotated, dest, spots, own, other, weight, left, right, bias, cosine, sine, slots, text
):
    step = pl.program_id(0)
    total = product(own, other, weight)
    total = total + left[...].astype(jnp.float32) + right[...].astype(jnp.float32) + bias[...]
    heads = []
    for head in range(2):
        values = total[:, head * HD : (head + 1) * HD]
        if head < rotated:
            values = values * cosine[...] + pltpu.roll(values, HD // 2, 1) * sine[...]
        heads.append(values.astype(jnp.bfloat16))

    @pl.when(step < BLOCKS - 1)
    def _():
        for head in range(2):
            slots[0, :, head * HD : (head + 1) * HD] = heads[head]

    @pl.when(step == BLOCKS - 1)
    def _():
        for head in range(2):
            text[:, head * HD : (head + 1) * HD] = heads[head]


def finish(rotated, dest, spots, own, other, weight, place, left, right, bias, cosine, sine, shards):
    def row(i, d, s):
        return (i, 0)

    def spot(i, d, s):
        return (s[i], 0)

    def none(i, d, s):
        return (0, 0)

    grid_spec = pltpu.PrefetchScalarGridSpec(
        num_scalar_prefetch=2,
        grid=(BLOCKS,),
        in_specs=[
            pl.BlockSpec((TILE, PART), row),
            pl.BlockSpec((TILE, PART), row),
            pl.BlockSpec((1, SLICE, WIDE), lambda i, d, s: place),
            pl.BlockSpec((TILE, WIDE), row),
            pl.BlockSpec((TILE, WIDE), row),
            pl.BlockSpec((1, WIDE), none),
            pl.BlockSpec((TILE, HD), spot),
            pl.BlockSpec((TILE, HD), spot),
        ],
        out_specs=[
            pl.BlockSpec((1, TILE, WIDE), lambda i, d, s: (d[i], 0, 0)),
            pl.BlockSpec((TILE, WIDE), none),
        ],
    )

    def body(*refs):
        finish_kernel(rotated, *refs)

    return pl.pallas_call(
        body,
        grid_spec=grid_spec,
        out_shape=[
            jax.ShapeDtypeStruct((shards, TILE, WIDE), jnp.bfloat16),
            jax.ShapeDtypeStruct((TILE, WIDE), jnp.bfloat16),
        ],
        compiler_params=params(),
        cost_estimate=cost(2 * SEQ * SLICE * WIDE, 2 * SEQ * SLICE),
        name="finish_rows",
    )(dest, spots, own, other, weight, left, right, bias, cosine, sine)


def attend_kernel(
    has_base, source, text_at, ends, slots, text, pair_slots, pair_text, *rest
):
    base, out, keys, values = rest if has_base else (None,) + rest
    block = pl.program_id(0)

    @pl.when(block == 0)
    def _():
        for at in range(BLOCKS):
            rows = slice(at * TILE, (at + 1) * TILE)

            @pl.when(text_at[0] == at)
            def _():
                keys[rows] = pair_text[:, :HD]
                values[rows] = pair_text[:, HD:]

            @pl.when(text_at[0] != at)
            def _():
                keys[rows] = pair_slots[source[at], :, :HD]
                values[rows] = pair_slots[source[at], :, HD:]

    queries = jnp.where(block == text_at[0], text[...], slots[0])
    queries = jnp.concatenate([queries[:, :HD], queries[:, HD:]], axis=0)
    score_scale = 1.0 / math.sqrt(HD)
    first = block * TILE
    index = lax.broadcasted_iota(jnp.int32, (2 * TILE, 1), 0)
    position = first + jnp.where(index >= TILE, index - TILE, index)
    start = jnp.zeros_like(position)
    low = jnp.int32(0)
    for at in range(4):
        end = ends[at]
        start = jnp.where(position >= end, end, start)
        low = jnp.where(first >= end, end, low)
    column = lax.broadcasted_iota(jnp.int32, (2 * TILE, TILE), 1)

    def scores_of(at):
        offset = pl.multiple_of(at * TILE, TILE)
        key_block = keys[pl.ds(offset, TILE), :]
        return (
            lax.dot_general(
                queries, key_block, (((1,), (1,)), ((), ())), preferred_element_type=jnp.float32
            )
            * score_scale
        )

    def mix(weights, at):
        offset = pl.multiple_of(at * TILE, TILE)
        return jnp.dot(
            weights.astype(jnp.bfloat16),
            values[pl.ds(offset, TILE), :],
            preferred_element_type=jnp.float32,
        )

    allowed = (column + first <= position) & (column + first >= start)
    scores = jnp.where(allowed, scores_of(block), masked_score)
    top = jnp.max(scores, axis=1, keepdims=True)
    weights = jnp.exp(scores - top)
    total = jnp.sum(weights, axis=1, keepdims=True)
    mixed = mix(weights, block)

    def body(at, carry):
        top, total, mixed = carry
        scores = jnp.where(column + at * TILE >= start, scores_of(at), masked_score)
        higher = jnp.maximum(top, jnp.max(scores, axis=1, keepdims=True))
        fade = jnp.exp(top - higher)
        weights = jnp.exp(scores - higher)
        total = total * fade + jnp.sum(weights, axis=1, keepdims=True)
        return higher, total, mixed * fade + mix(weights, at)

    top, total, mixed = lax.fori_loop(low // TILE, block, body, (top, total, mixed))
    result = (mixed / total).astype(jnp.bfloat16)
    out[:, :HD] = result[:TILE]
    out[:, HD:] = result[TILE:]


def attend(source, text_at, ends, slots, text, pair_slots, pair_text, base, half):
    shards = pair_slots.shape[0]
    in_specs = [
        pl.BlockSpec((1, TILE, WIDE), lambda i, s, t, e: (s[i], 0, 0)),
        pl.BlockSpec((TILE, WIDE), lambda i, s, t, e: (0, 0)),
        pl.BlockSpec((shards, TILE, WIDE), lambda i, s, t, e: (0, 0, 0)),
        pl.BlockSpec((TILE, WIDE), lambda i, s, t, e: (0, 0)),
    ]
    operands = [source, text_at, ends, slots, text, pair_slots, pair_text]
    aliases = {}
    if base is not None:
        in_specs.append(pl.BlockSpec(memory_space=pl.ANY))
        operands.append(base)
        aliases = {7: 0}
    grid_spec = pltpu.PrefetchScalarGridSpec(
        num_scalar_prefetch=3,
        grid=(BLOCKS,),
        in_specs=in_specs,
        out_specs=pl.BlockSpec((TILE, WIDE), lambda i, s, t, e: (i, half)),
        scratch_shapes=[
            pltpu.VMEM((SEQ, HD), jnp.bfloat16),
            pltpu.VMEM((SEQ, HD), jnp.bfloat16),
        ],
    )

    def body(*refs):
        attend_kernel(base is not None, *refs)

    return pl.pallas_call(
        body,
        grid_spec=grid_spec,
        out_shape=jax.ShapeDtypeStruct((SEQ, 2 * WIDE), jnp.bfloat16),
        input_output_aliases=aliases,
        compiler_params=params(),
        cost_estimate=cost(4 * SEQ * SEQ * WIDE, 6 * SEQ * WIDE, SEQ * SEQ),
        name="attend",
    )(*operands)


def local(
    text_rows,
    vis_rows,
    q_weight,
    kv_weight,
    q_bias,
    kv_bias,
    norm_gain,
    tile_dest,
    tile_block,
    doc_lens,
):
    width = norm_gain.shape[0]
    shards = lax.axis_size("dp")
    me = lax.axis_index("dp")
    tensor_at = lax.axis_index("tensor")
    x_at, high = tensor_at // 2, tensor_at % 2

    owner_ids = jnp.arange(shards, dtype=jnp.int32)
    source_of = jnp.sum(jnp.where(tile_dest == me, owner_ids[:, None], 0), axis=0)
    my_dest = lax.dynamic_slice_in_dim(tile_dest, me, 1, 0)[0]
    blocks = tile_block[0]
    text_block = sum(range(BLOCKS)) - jnp.sum(blocks)
    all_blocks = lax.all_gather(tile_block, "dp", axis=0, tiled=True)
    sent = (owner_ids[:, None] == my_dest[None, :]).astype(jnp.int32)
    spots = jnp.concatenate([jnp.sum(sent * all_blocks, axis=0), text_block[None]])
    dest = jnp.concatenate([my_dest, my_dest[-1:]])
    at_block = blocks[None, :] == jnp.arange(BLOCKS, dtype=jnp.int32)[:, None]
    source = jnp.sum(jnp.where(at_block, source_of[None, :], 0), axis=1)
    text_at = text_block[None]
    ends = jnp.cumsum(doc_lens[0])

    text_own = lax.dynamic_slice_in_dim(text_rows, text_block * TILE, TILE, 0)
    vis_other = swap_high(vis_rows)
    text_other = swap_high(text_own)

    q_all = lax.all_gather(transpose_weight(q_weight), "dp", axis=0, tiled=True)
    q_all = q_all.reshape(4, SLICE, q_weight.shape[1])
    pairs = kv_weight.reshape(4, 2, PART, WIDE)

    def pair_slice(step):
        rows = lax.dynamic_index_in_dim(pairs, (x_at + step) % 4, 0, keepdims=False)
        first = lax.dynamic_index_in_dim(rows, high, 0, keepdims=False)
        second = lax.dynamic_index_in_dim(rows, 1 - high, 0, keepdims=False)
        return jnp.concatenate([first, second], axis=0)

    pair_weights = [pair_slice(0)] + [shift_x(pair_slice(4 - r), 4 - r) for r in range(1, 4)]
    pair_weights = [weight[None] for weight in pair_weights]

    def squares(rows):
        floats = rows.astype(jnp.float32)
        return jnp.sum(floats * floats, axis=1)

    spread = jnp.concatenate([squares(vis_rows), squares(text_own)])
    spread = lax.psum(spread, "tensor") / width
    scale = lax.rsqrt(spread + eps)[:, None]
    gains = norm_gain.reshape(8, 1, PART)
    gain_own = lax.dynamic_index_in_dim(gains, tensor_at, 0, keepdims=False)
    gain_other = lax.dynamic_index_in_dim(gains, tensor_at ^ 1, 0, keepdims=False)
    own = norm_rows(text_at, vis_rows, text_rows, scale, gain_own)
    other = norm_rows(jnp.zeros((1,), jnp.int32), vis_other, text_other, scale, gain_other)

    cosine, sine = rope_tables(SEQ, HD)
    chunks = [
        (1, [(weight, (0, 0, 0)) for weight in pair_weights], kv_bias.reshape(1, WIDE)),
        (2, [(q_all, (r, 0, 0)) for r in range(4)], q_bias[None, :WIDE]),
        (2, [(q_all, (r, 0, 1)) for r in range(4)], q_bias[None, WIDE:]),
    ]
    routed = []
    for rotated, weights, bias in chunks:
        far_up, far_down = far_parts(own, other, *weights[2])
        got_up, got_down = shift_x(far_up, 1), shift_x(far_down, 3)
        up, down = near_parts(own, other, *weights[1], *weights[3], got_up, got_down)
        left, right = shift_x(up, 1), shift_x(down, 3)
        slots, text = finish(
            rotated, dest, spots, own, other, *weights[0], left, right, bias, cosine, sine, shards
        )
        routed.append((lax.all_to_all(slots, "dp", split_axis=0, concat_axis=0, tiled=True), text))
    context = None
    for half in range(2):
        context = attend(source, text_at, ends, *routed[1 + half], *routed[0], context, half)
    return context


def solution(mesh):
    in_specs = (
        P("dp", "tensor"),
        P("dp", "tensor"),
        P("dp", "tensor"),
        P(None, None, "tensor"),
        P("tensor"),
        P(None, "tensor"),
        P(),
        P(),
        P("dp", None),
        P("dp", None),
    )
    out_specs = P("dp", "tensor")
    return jax.shard_map(local, mesh=mesh, in_specs=in_specs, out_specs=out_specs, check_vma=False)
```

```python
import functools
import math

import jax
import jax.numpy as jnp
from jax import lax
from jax.experimental import pallas as pl
from jax.experimental.pallas import tpu as pltpu
from jax.sharding import PartitionSpec as P

HD = 128
TILE = 256
BLOCKS = 7
SEQ = BLOCKS * TILE
PART = 1024
SLICE = 2 * PART
CORE_PART = PART // 2
WIDE = 2 * HD
ROWS = SEQ // 4
VMEM = 48 * 1024 * 1024

rope_base = 1000000.0
eps = 1e-06
masked_score = -1e30


def params():
    return pltpu.CompilerParams(vmem_limit_bytes=VMEM)


def cost(flops, moved, transcendentals=0):
    return pl.CostEstimate(flops=flops, bytes_accessed=moved, transcendentals=transcendentals)


def rope_tables(length, width):
    half_width = width // 2
    inverse = rope_base ** (-(jnp.arange(half_width, dtype=jnp.float32) * 2.0) / width)
    angles = jnp.arange(length, dtype=jnp.float32)[:, None] * inverse[None, :]
    cosine, sine = jnp.cos(angles), jnp.sin(angles)
    return (
        jnp.concatenate([cosine, cosine], axis=1),
        jnp.concatenate([-sine, sine], axis=1),
    )


def shift_x(value, step):
    pairs = [
        (2 * x + high, 2 * ((x + step) % 4) + high) for x in range(4) for high in range(2)
    ]
    return lax.ppermute(value, "tensor", pairs)


def swap_tensor(value, bits):
    return lax.ppermute(value, "tensor", [(t, t ^ bits) for t in range(8)])


def swap_dp(value, bits):
    return lax.ppermute(value, "dp", [(d, d ^ bits) for d in range(16)])


def shift_z(value, step):
    return lax.ppermute(value, "dp", [(d, (d + 4 * step) % 16) for d in range(16)])


def place(z, low, core, x, high):
    return ((z * 2 + low) * 2 + core) * 8 + x * 2 + high


def all_places():
    return [
        (z, low, core, x, high)
        for z in range(4)
        for low in range(2)
        for core in range(2)
        for x in range(4)
        for high in range(2)
    ]


def ring_x(value):
    pairs = [
        (place(z, low, core, x, high), place(z, low, core, (x + 1 - 2 * core) % 4, high))
        for z, low, core, x, high in all_places()
    ]
    return lax.ppermute(value, ("dp", "tensor"), pairs)


def mirror_z(value):
    pairs = [
        (place(z, low, core, x, high), place((x - z) % 4, low, core, x, high))
        for z, low, core, x, high in all_places()
    ]
    return lax.ppermute(value, ("dp", "tensor"), pairs)


def slide_x(value):
    pairs = [
        (place(z, low, core, x, high), place(z, low, core, (x - z) % 4, high))
        for z, low, core, x, high in all_places()
    ]
    return lax.ppermute(value, ("dp", "tensor"), pairs)


def lock(values, guards):
    return lax.optimization_barrier((tuple(values), tuple(guards)))[0]


def norm_kernel(bounds, begin, picks, *refs):
    parts, scale, gain, out = refs[: len(bounds)], refs[len(bounds)], refs[len(bounds) + 1], refs[-1]
    step = pl.program_id(0) + begin
    core = picks[1]

    def put(rows):
        result = (rows[...].astype(jnp.float32) * scale[...] * gain[...]).astype(jnp.bfloat16)
        front, back = result[:, :CORE_PART], result[:, CORE_PART:]

        @pl.when(core == 0)
        def _():
            out[:, :CORE_PART] = front
            out[:, CORE_PART:] = back

        @pl.when(core == 1)
        def _():
            out[:, :CORE_PART] = back
            out[:, CORE_PART:] = front

    for part, (first, last) in zip(parts, bounds):
        pl.when((step >= first) & (step < last))(functools.partial(put, part))


def norm_rows(picks, parts, bounds, scale, gain, base=None):
    begin, end = bounds[0][0], bounds[-1][1]

    def spec(part, first, last):
        if part.shape[0] == SEQ:
            return pl.BlockSpec((TILE, PART), lambda i, s: (s[0], 0))
        return pl.BlockSpec(
            (TILE, PART), lambda i, s: (jnp.clip(i + begin - first, 0, last - first - 1), 0)
        )

    aliased = [] if base is None else [base]
    grid_spec = pltpu.PrefetchScalarGridSpec(
        num_scalar_prefetch=1,
        grid=(end - begin,),
        in_specs=[spec(part, *bound) for part, bound in zip(parts, bounds)]
        + [
            pl.BlockSpec((TILE, 1), lambda i, s: (i + begin, 0)),
            pl.BlockSpec((1, PART), lambda i, s: (0, 0)),
        ]
        + later(aliased),
        out_specs=pl.BlockSpec((TILE, PART), lambda i, s: (i + begin, 0)),
    )
    rows = (end - begin) * TILE
    return pl.pallas_call(
        functools.partial(norm_kernel, bounds, begin),
        grid_spec=grid_spec,
        out_shape=jax.ShapeDtypeStruct((SEQ, PART), jnp.bfloat16),
        input_output_aliases={len(parts) + 3: 0} if aliased else {},
        compiler_params=params(),
        cost_estimate=cost(3 * rows * PART, 4 * rows * PART),
        name="norm_rows",
    )(picks, *parts, scale, gain, *aliased)


def later(tokens):
    return [pl.BlockSpec(memory_space=pl.ANY)] * len(tokens)


def part_kernel(at, own, other, kv_mine, kv_theirs, q_mine, q_theirs, *rest):
    kv_out, first_out, second_out = rest[-3:]

    def product(mine, theirs):
        total = None
        for columns, part in ((slice(0, CORE_PART), mine), (slice(CORE_PART, PART), theirs)):
            for rows, at in ((own, slice(0, CORE_PART)), (other, slice(CORE_PART, PART))):
                term = jnp.dot(rows[:, columns], part[0, at], preferred_element_type=jnp.float32)
                total = term if total is None else total + term
        return total

    kv_out[...] = product(kv_mine, kv_theirs).astype(kv_out.dtype)
    queries = product(q_mine, q_theirs).astype(first_out.dtype)
    first_out[...] = queries[:, :WIDE]
    second_out[...] = queries[:, WIDE:]


def part_of(at, own, other, kv_mine, kv_theirs, q_mine, q_theirs, dtype, tokens):
    grid_spec = pltpu.PrefetchScalarGridSpec(
        num_scalar_prefetch=1,
        grid=(SEQ // ROWS,),
        in_specs=[
            pl.BlockSpec((ROWS, PART), lambda i, s: (i, 0)),
            pl.BlockSpec((ROWS, PART), lambda i, s: (i, 0)),
            pl.BlockSpec((1, PART, WIDE), lambda i, s: (s[0], 0, 0)),
            pl.BlockSpec((1, PART, WIDE), lambda i, s: (s[0], 0, 0)),
            pl.BlockSpec((1, PART, 2 * WIDE), lambda i, s: (s[1], 0, 0)),
            pl.BlockSpec((1, PART, 2 * WIDE), lambda i, s: (s[1], 0, 0)),
            *later(tokens),
        ],
        out_specs=[pl.BlockSpec((ROWS, WIDE), lambda i, s: (i, 0))] * 3,
    )
    return pl.pallas_call(
        part_kernel,
        grid_spec=grid_spec,
        out_shape=[jax.ShapeDtypeStruct((SEQ, WIDE), dtype)] * 3,
        compiler_params=params(),
        cost_estimate=cost(6 * SEQ * SLICE * WIDE, 2 * SEQ * SLICE),
        name="part_rows",
    )(at, own, other, kv_mine, kv_theirs, q_mine, q_theirs, *tokens)


def finish_kernel(rotated, dest, spots, here, got, bias, cosine, sine, slots, text):
    step = pl.program_id(0)
    total = here[...].astype(jnp.float32) + got[...].astype(jnp.float32) + bias[...]
    heads = []
    for head in range(2):
        values = total[:, head * HD : (head + 1) * HD]
        if head < rotated:
            values = values * cosine[...] + pltpu.roll(values, HD // 2, 1) * sine[...]
        heads.append(values.astype(jnp.bfloat16))

    @pl.when(step < BLOCKS - 1)
    def _():
        for head in range(2):
            slots[0, :, head * HD : (head + 1) * HD] = heads[head]

    @pl.when(step == BLOCKS - 1)
    def _():
        for head in range(2):
            text[:, head * HD : (head + 1) * HD] = heads[head]


def finish(rotated, dest, spots, here, got, bias, tables, shards):
    def row(i, d, s):
        return (i, 0)

    def spot(i, d, s):
        return (s[i], 0)

    def none(i, d, s):
        return (0, 0)

    grid_spec = pltpu.PrefetchScalarGridSpec(
        num_scalar_prefetch=2,
        grid=(BLOCKS,),
        in_specs=[
            pl.BlockSpec((TILE, WIDE), row),
            pl.BlockSpec((TILE, WIDE), row),
            pl.BlockSpec((1, WIDE), none),
            pl.BlockSpec((TILE, HD), spot),
            pl.BlockSpec((TILE, HD), spot),
        ],
        out_specs=[
            pl.BlockSpec((1, TILE, WIDE), lambda i, d, s: (d[i], 0, 0)),
            pl.BlockSpec((TILE, WIDE), none),
        ],
    )
    return pl.pallas_call(
        functools.partial(finish_kernel, rotated),
        grid_spec=grid_spec,
        out_shape=[
            jax.ShapeDtypeStruct((shards, TILE, WIDE), jnp.bfloat16),
            jax.ShapeDtypeStruct((TILE, WIDE), jnp.bfloat16),
        ],
        compiler_params=params(),
        cost_estimate=cost(8 * SEQ * WIDE, 10 * SEQ * WIDE),
        name="finish_rows",
    )(dest, spots, here, got, bias, *tables)


def attend_kernel(
    has_base, source, text_at, ends, slots, text, pair_slots, pair_text, *rest
):
    base, out, keys, values = rest if has_base else (None,) + rest
    block = pl.program_id(0)

    @pl.when(block == 0)
    def _():
        for at in range(BLOCKS):
            rows = slice(at * TILE, (at + 1) * TILE)

            @pl.when(text_at[0] == at)
            def _():
                keys[rows] = pair_text[:, :HD]
                values[rows] = pair_text[:, HD:]

            @pl.when(text_at[0] != at)
            def _():
                keys[rows] = pair_slots[source[at], :, :HD]
                values[rows] = pair_slots[source[at], :, HD:]

    queries = jnp.where(block == text_at[0], text[...], slots[0])
    queries = jnp.concatenate([queries[:, :HD], queries[:, HD:]], axis=0)
    score_scale = 1.0 / math.sqrt(HD)
    first = block * TILE
    index = lax.broadcasted_iota(jnp.int32, (2 * TILE, 1), 0)
    position = first + jnp.where(index >= TILE, index - TILE, index)
    start = jnp.zeros_like(position)
    low = jnp.int32(0)
    for at in range(4):
        end = ends[at]
        start = jnp.where(position >= end, end, start)
        low = jnp.where(first >= end, end, low)
    column = lax.broadcasted_iota(jnp.int32, (2 * TILE, TILE), 1)

    def scores_of(at):
        offset = pl.multiple_of(at * TILE, TILE)
        key_block = keys[pl.ds(offset, TILE), :]
        return (
            lax.dot_general(
                queries, key_block, (((1,), (1,)), ((), ())), preferred_element_type=jnp.float32
            )
            * score_scale
        )

    def mix(weights, at):
        offset = pl.multiple_of(at * TILE, TILE)
        return jnp.dot(
            weights.astype(jnp.bfloat16),
            values[pl.ds(offset, TILE), :],
            preferred_element_type=jnp.float32,
        )

    allowed = (column + first <= position) & (column + first >= start)
    scores = jnp.where(allowed, scores_of(block), masked_score)
    top = jnp.max(scores, axis=1, keepdims=True)
    weights = jnp.exp(scores - top)
    total = jnp.sum(weights, axis=1, keepdims=True)
    mixed = mix(weights, block)

    def body(at, carry):
        top, total, mixed = carry
        scores = jnp.where(column + at * TILE >= start, scores_of(at), masked_score)
        higher = jnp.maximum(top, jnp.max(scores, axis=1, keepdims=True))
        fade = jnp.exp(top - higher)
        weights = jnp.exp(scores - higher)
        total = total * fade + jnp.sum(weights, axis=1, keepdims=True)
        return higher, total, mixed * fade + mix(weights, at)

    top, total, mixed = lax.fori_loop(low // TILE, block, body, (top, total, mixed))
    result = (mixed / total).astype(jnp.bfloat16)
    out[:, :HD] = result[:TILE]
    out[:, HD:] = result[TILE:]


def attend(source, text_at, ends, slots, text, pair_slots, pair_text, base, half):
    shards = pair_slots.shape[0]
    in_specs = [
        pl.BlockSpec((1, TILE, WIDE), lambda i, s, t, e: (s[i], 0, 0)),
        pl.BlockSpec((TILE, WIDE), lambda i, s, t, e: (0, 0)),
        pl.BlockSpec((shards, TILE, WIDE), lambda i, s, t, e: (0, 0, 0)),
        pl.BlockSpec((TILE, WIDE), lambda i, s, t, e: (0, 0)),
    ]
    operands = [source, text_at, ends, slots, text, pair_slots, pair_text]
    aliases = {}
    if base is not None:
        in_specs.append(pl.BlockSpec(memory_space=pl.ANY))
        operands.append(base)
        aliases = {7: 0}
    grid_spec = pltpu.PrefetchScalarGridSpec(
        num_scalar_prefetch=3,
        grid=(BLOCKS,),
        in_specs=in_specs,
        out_specs=pl.BlockSpec((TILE, WIDE), lambda i, s, t, e: (i, half)),
        scratch_shapes=[
            pltpu.VMEM((SEQ, HD), jnp.bfloat16),
            pltpu.VMEM((SEQ, HD), jnp.bfloat16),
        ],
    )

    def body(*refs):
        attend_kernel(base is not None, *refs)

    return pl.pallas_call(
        body,
        grid_spec=grid_spec,
        out_shape=jax.ShapeDtypeStruct((SEQ, 2 * WIDE), jnp.bfloat16),
        input_output_aliases=aliases,
        compiler_params=params(),
        cost_estimate=cost(4 * SEQ * SEQ * WIDE, 6 * SEQ * WIDE, SEQ * SEQ),
        name="attend",
    )(*operands)


def local(
    text_rows,
    vis_rows,
    q_weight,
    kv_weight,
    q_bias,
    kv_bias,
    norm_gain,
    tile_dest,
    tile_block,
    doc_lens,
):
    width = norm_gain.shape[0]
    shards = lax.axis_size("dp")
    me = lax.axis_index("dp")
    tensor_at = lax.axis_index("tensor")
    x_at, high = tensor_at // 2, tensor_at % 2
    z_at, low, core = me // 4, me // 2 % 2, me % 2
    blocks = tile_block[0]
    text_block = sum(range(BLOCKS)) - jnp.sum(blocks)

    def squares(rows):
        floats = rows.astype(jnp.float32)
        return jnp.sum(floats * floats, axis=1)

    pieces = kv_weight.reshape(4, 2, 2, CORE_PART, WIDE)

    def piece(step, core_at):
        rows = lax.dynamic_index_in_dim(pieces, (x_at + step) % 4, 0, keepdims=False)
        rows = lax.dynamic_index_in_dim(rows, core_at, 1, keepdims=False)
        first = lax.dynamic_index_in_dim(rows, high, 0, keepdims=False)
        second = lax.dynamic_index_in_dim(rows, 1 - high, 0, keepdims=False)
        return jnp.concatenate([first, second], axis=0)

    firsts = [vis_rows[at * TILE : (at + 1) * TILE] for at in range(3)]
    text_own = lax.dynamic_slice_in_dim(text_rows, text_block * TILE, TILE, 0)
    last = jnp.concatenate([vis_rows[3 * TILE :], text_own], axis=0)
    spread = jnp.concatenate([squares(vis_rows), squares(text_own)]).reshape(BLOCKS, TILE)

    q_here = mirror_z(q_weight)
    others = [swap_tensor(firsts[0], 1)]
    spread = spread + swap_tensor(spread, 2)
    gathered = jnp.concatenate([tile_block, swap_dp(tile_block, 2)], axis=0)

    q_here, firsts[1], spread, gathered = lock((q_here, firsts[1], spread, gathered), others)
    q_here = slide_x(q_here)
    others.append(swap_tensor(firsts[1], 1))
    spread = spread + swap_tensor(spread, 4)
    gathered = jnp.concatenate([gathered, swap_dp(gathered, 1)], axis=0)

    q_here, firsts[2], spread, gathered, kv_up, kv_down = lock(
        (q_here, firsts[2], spread, gathered, piece(1, core), piece(3, core)), others
    )
    q_low = swap_dp(q_here, 2)
    others.append(swap_tensor(firsts[2], 1))
    spread = spread + swap_tensor(spread, 1)
    kv_third = shift_x(kv_up, 1)
    kv_first = shift_x(kv_down, 3)

    own_half = low == high
    q_pair = jnp.concatenate(
        [jnp.where(own_half, q_here, q_low), jnp.where(own_half, q_low, q_here)], axis=0
    )
    q_pair, last, spread, gathered, kv_far = lock(
        (q_pair, last, spread, gathered, piece(2, core)), (*others, kv_first, kv_third)
    )
    other_last = swap_tensor(last, 1)
    q_mine = jnp.stack([q_pair] + [shift_z(q_pair, step) for step in range(1, 4)])
    kv_second = shift_x(kv_far, 2)
    kv_mine = jnp.stack([piece(0, core), kv_first, kv_second, kv_third])

    q_mine, kv_mine, gathered = lock((q_mine, kv_mine, gathered), (other_last,))
    q_theirs = swap_dp(q_mine, 1)
    kv_theirs = swap_dp(kv_mine, 1)
    for bits in (4, 8):
        gathered = jnp.concatenate([gathered, swap_dp(gathered, bits)], axis=0)
    order = [0]
    for bits in (2, 1, 4, 8):
        order = order + [entry ^ bits for entry in order]

    owner_ids = jnp.arange(shards, dtype=jnp.int32)
    source_of = jnp.sum(jnp.where(tile_dest == me, owner_ids[:, None], 0), axis=0)
    my_dest = lax.dynamic_slice_in_dim(tile_dest, me, 1, 0)[0]
    sent = (me ^ jnp.array(order, jnp.int32))[:, None] == my_dest[None, :]
    spots = jnp.concatenate([jnp.sum(jnp.where(sent, gathered, 0), axis=0), text_block[None]])
    dest = jnp.concatenate([my_dest, my_dest[-1:]])
    at_block = blocks[None, :] == jnp.arange(BLOCKS, dtype=jnp.int32)[:, None]
    source = jnp.sum(jnp.where(at_block, source_of[None, :], 0), axis=1)
    text_at = text_block[None]
    ends = jnp.cumsum(doc_lens[0])

    scale = lax.rsqrt(spread / width + eps).reshape(SEQ, 1)
    gains = norm_gain.reshape(8, 1, PART)
    gain_own = lax.dynamic_index_in_dim(gains, tensor_at, 0, keepdims=False)
    gain_other = lax.dynamic_index_in_dim(gains, tensor_at ^ 1, 0, keepdims=False)
    own = norm_rows(
        jnp.stack([text_block, core]), (vis_rows, text_rows), ((0, 6), (6, 7)), scale, gain_own
    )
    plain = jnp.stack([jnp.int32(0), core])
    other = norm_rows(plain, others, ((0, 1), (1, 2), (2, 3)), scale, gain_other)
    other = norm_rows(plain, (other_last,), ((3, 7),), scale, gain_other, other)

    def part(turn, dtype, tokens):
        group = jnp.where(core == 0, (4 - turn) % 4, turn)
        at = jnp.stack([group, (z_at - group) % 4]).astype(jnp.int32)
        return part_of(at, own, other, kv_mine, kv_theirs, q_mine, q_theirs, dtype, tokens)

    def add(here, got):
        return (here.astype(jnp.float32) + got.astype(jnp.float32)).astype(jnp.bfloat16)

    first = part(1, jnp.bfloat16, [])
    second = part(2, jnp.bfloat16, first[:1])
    third = part(3, jnp.bfloat16, second[:1])
    here = part(0, jnp.float32, third[:1])
    tables = rope_tables(SEQ, HD)
    chunks = [
        (1, kv_bias.reshape(1, WIDE)),
        (2, q_bias[None, :WIDE]),
        (2, q_bias[None, WIDE:]),
    ]
    moving = [ring_x(rows) for rows in first]
    for parts in (second, third):
        for at in range(3):
            moving[at] = ring_x(add(parts[at], moving[at]))
    routed = []
    for at, (rotated, bias) in enumerate(chunks):
        slots, text = finish(rotated, dest, spots, here[at], moving[at], bias, tables, shards)
        arrived = lax.all_to_all(slots, "dp", split_axis=0, concat_axis=0, tiled=True)
        routed.append((arrived, text))
    context = None
    for half in range(2):
        context = attend(source, text_at, ends, *routed[1 + half], *routed[0], context, half)
    return context


def solution(mesh):
    in_specs = (
        P("dp", "tensor"),
        P("dp", "tensor"),
        P("dp", "tensor"),
        P(None, None, "tensor"),
        P("tensor"),
        P(None, "tensor"),
        P(),
        P(),
        P("dp", None),
        P("dp", None),
    )
    out_specs = P("dp", "tensor")
    return jax.shard_map(local, mesh=mesh, in_specs=in_specs, out_specs=out_specs, check_vma=False)
```

```python
import functools
import math

import jax
import jax.numpy as jnp
from jax import lax
from jax.experimental import pallas as pl
from jax.experimental.pallas import tpu as pltpu
from jax.sharding import PartitionSpec as P

HD = 128
TILE = 256
BLOCKS = 7
SEQ = BLOCKS * TILE
PART = 1024
SLICE = 2 * PART
CORE_PART = PART // 2
TAIL = 16
WIDE = 2 * HD
ROWS = SEQ // 4
VMEM = 48 * 1024 * 1024

rope_base = 1000000.0
eps = 1e-06
masked_score = -1e30


def params():
    return pltpu.CompilerParams(vmem_limit_bytes=VMEM)


def cost(flops, moved, transcendentals=0):
    return pl.CostEstimate(flops=flops, bytes_accessed=moved, transcendentals=transcendentals)


def rope_tables(length, width):
    half_width = width // 2
    inverse = rope_base ** (-(jnp.arange(half_width, dtype=jnp.float32) * 2.0) / width)
    angles = jnp.arange(length, dtype=jnp.float32)[:, None] * inverse[None, :]
    cosine, sine = jnp.cos(angles), jnp.sin(angles)
    return (
        jnp.concatenate([cosine, cosine], axis=1),
        jnp.concatenate([-sine, sine], axis=1),
    )


def shift_x(value, step):
    pairs = [
        (2 * x + high, 2 * ((x + step) % 4) + high) for x in range(4) for high in range(2)
    ]
    return lax.ppermute(value, "tensor", pairs)


def swap_tensor(value, bits):
    return lax.ppermute(value, "tensor", [(t, t ^ bits) for t in range(8)])


def swap_dp(value, bits):
    return lax.ppermute(value, "dp", [(d, d ^ bits) for d in range(16)])


def place(z, low, core, x, high):
    return ((z * 2 + low) * 2 + core) * 8 + x * 2 + high


def all_places():
    return [
        (z, low, core, x, high)
        for z in range(4)
        for low in range(2)
        for core in range(2)
        for x in range(4)
        for high in range(2)
    ]


def ring_x(value):
    pairs = [
        (place(z, low, core, x, high), place(z, low, core, (x + 1 - 2 * core) % 4, high))
        for z, low, core, x, high in all_places()
    ]
    return lax.ppermute(value, ("dp", "tensor"), pairs)


def shift_z(value, step):
    return lax.ppermute(value, "dp", [(d, (d + 4 * step) % 16) for d in range(16)])


def mirror_z(value):
    pairs = [
        (place(z, low, core, x, high), place((x - z) % 4, low, core, x, high))
        for z, low, core, x, high in all_places()
    ]
    return lax.ppermute(value, ("dp", "tensor"), pairs)


def slide_x(value):
    pairs = [
        (place(z, low, core, x, high), place(z, low, core, (x - z) % 4, high))
        for z, low, core, x, high in all_places()
    ]
    return lax.ppermute(value, ("dp", "tensor"), pairs)


def lock(values, guards):
    return lax.optimization_barrier((tuple(values), tuple(guards)))[0]


def norm_kernel(bounds, begin, picks, *refs):
    parts, scale, gain, out = refs[: len(bounds)], refs[len(bounds)], refs[len(bounds) + 1], refs[-1]
    step = pl.program_id(0) + begin
    core = picks[1]

    def put(rows):
        result = (rows[...].astype(jnp.float32) * scale[...] * gain[...]).astype(jnp.bfloat16)
        front, back = result[:, :CORE_PART], result[:, CORE_PART:]

        @pl.when(core == 0)
        def _():
            out[:, :CORE_PART] = front
            out[:, CORE_PART:] = back

        @pl.when(core == 1)
        def _():
            out[:, :CORE_PART] = back
            out[:, CORE_PART:] = front

    for part, (first, last) in zip(parts, bounds):
        pl.when((step >= first) & (step < last))(functools.partial(put, part))


def norm_rows(picks, parts, bounds, scale, gain, base=None):
    begin, end = bounds[0][0], bounds[-1][1]

    def spec(part, first, last):
        if part.shape[0] == SEQ:
            return pl.BlockSpec((TILE, PART), lambda i, s: (s[0], 0))
        return pl.BlockSpec(
            (TILE, PART), lambda i, s: (jnp.clip(i + begin - first, 0, last - first - 1), 0)
        )

    aliased = [] if base is None else [base]
    grid_spec = pltpu.PrefetchScalarGridSpec(
        num_scalar_prefetch=1,
        grid=(end - begin,),
        in_specs=[spec(part, *bound) for part, bound in zip(parts, bounds)]
        + [
            pl.BlockSpec((TILE, 1), lambda i, s: (i + begin, 0)),
            pl.BlockSpec((1, PART), lambda i, s: (0, 0)),
        ]
        + later(aliased),
        out_specs=pl.BlockSpec((TILE, PART), lambda i, s: (i + begin, 0)),
    )
    rows = (end - begin) * TILE
    return pl.pallas_call(
        functools.partial(norm_kernel, bounds, begin),
        grid_spec=grid_spec,
        out_shape=jax.ShapeDtypeStruct((SEQ, PART), jnp.bfloat16),
        input_output_aliases={len(parts) + 3: 0} if aliased else {},
        compiler_params=params(),
        cost_estimate=cost(0, 0),
        name="norm_rows",
    )(picks, *parts, scale, gain, *aliased)


def later(tokens):
    return [pl.BlockSpec(memory_space=pl.ANY)] * len(tokens)


def part_kernel(count, at, own, other, *rest):
    weights, outs = rest[: 2 * count], rest[-count:]
    for turn in range(count):
        total = None
        for columns, part in zip(
            (slice(0, CORE_PART), slice(CORE_PART, PART)), weights[2 * turn : 2 * turn + 2]
        ):
            for rows, at in ((own, slice(0, CORE_PART)), (other, slice(CORE_PART, PART))):
                term = jnp.dot(rows[:, columns], part[0, at], preferred_element_type=jnp.float32)
                total = term if total is None else total + term
        outs[turn][...] = total.astype(outs[turn].dtype)


def parts_of(at, own, other, mine, theirs, half, dtypes, tokens):
    count = len(dtypes)

    def weight_spec(turn):
        return pl.BlockSpec((1, PART, WIDE), lambda i, s: (s[turn], 0, half))

    grid_spec = pltpu.PrefetchScalarGridSpec(
        num_scalar_prefetch=1,
        grid=(SEQ // ROWS,),
        in_specs=[
            pl.BlockSpec((ROWS, PART), lambda i, s: (i, 0)),
            pl.BlockSpec((ROWS, PART), lambda i, s: (i, 0)),
            *[weight_spec(turn) for turn in range(count) for _ in range(2)],
            *later(tokens),
        ],
        out_specs=[pl.BlockSpec((ROWS, WIDE), lambda i, s: (i, 0))] * count,
    )
    return pl.pallas_call(
        functools.partial(part_kernel, count),
        grid_spec=grid_spec,
        out_shape=[jax.ShapeDtypeStruct((SEQ, WIDE), dtype) for dtype in dtypes],
        compiler_params=params(),
        cost_estimate=cost(2 * count * SEQ * SLICE * WIDE, 2 * SEQ * SLICE),
        name="part_rows",
    )(at, own, other, *[mine, theirs] * count, *tokens)


def finish_kernel(rotated, dest, spots, *refs):
    count = len(rotated) // 2
    heres, gots, biases = refs[:count], refs[count : 2 * count], refs[2 * count : 3 * count]
    cosine, sine, slots, text = refs[3 * count :]
    step = pl.program_id(0)
    heads = []
    for at in range(count):
        total = heres[at][...] + gots[at][...].astype(jnp.float32) + biases[at][...]
        for head in range(2):
            values = total[:, head * HD : (head + 1) * HD]
            if rotated[2 * at + head]:
                values = values * cosine[...] + pltpu.roll(values, HD // 2, 1) * sine[...]
            heads.append(values.astype(jnp.bfloat16))

    @pl.when(step < BLOCKS - 1)
    def _():
        for head, values in enumerate(heads):
            slots[0, :, head * HD : (head + 1) * HD] = values

    @pl.when(step == BLOCKS - 1)
    def _():
        for head, values in enumerate(heads):
            text[:, head * HD : (head + 1) * HD] = values


def finish(rotated, dest, spots, heres, gots, biases, tables, shards):
    count = len(heres)

    def row(i, d, s):
        return (i, 0)

    def spot(i, d, s):
        return (s[i], 0)

    def none(i, d, s):
        return (0, 0)

    grid_spec = pltpu.PrefetchScalarGridSpec(
        num_scalar_prefetch=2,
        grid=(BLOCKS,),
        in_specs=[
            *[pl.BlockSpec((TILE, WIDE), row)] * (2 * count),
            *[pl.BlockSpec((1, WIDE), none)] * count,
            pl.BlockSpec((TILE, HD), spot),
            pl.BlockSpec((TILE, HD), spot),
        ],
        out_specs=[
            pl.BlockSpec((1, TILE, count * WIDE), lambda i, d, s: (d[i], 0, 0)),
            pl.BlockSpec((TILE, count * WIDE), none),
        ],
    )
    return pl.pallas_call(
        functools.partial(finish_kernel, rotated),
        grid_spec=grid_spec,
        out_shape=[
            jax.ShapeDtypeStruct((shards, TILE, count * WIDE), jnp.bfloat16),
            jax.ShapeDtypeStruct((TILE, count * WIDE), jnp.bfloat16),
        ],
        compiler_params=params(),
        cost_estimate=cost(8 * count * SEQ * WIDE, 10 * count * SEQ * WIDE),
        name="finish_rows",
    )(dest, spots, *heres, *gots, *biases, *tables)


def pair_kernel(source, text_at, slots, text, keys, values):
    block = pl.program_id(0)

    def put(rows):
        keys[...] = rows[:, :HD]
        values[:HD] = rows[:, HD:].T
        values[HD:] = jnp.ones((TAIL, TILE), jnp.bfloat16)

    @pl.when(text_at[0] == block)
    def _():
        put(text[...])

    @pl.when(text_at[0] != block)
    def _():
        put(slots[0])


def gather_pair(source, text_at, slots, text):
    grid_spec = pltpu.PrefetchScalarGridSpec(
        num_scalar_prefetch=2,
        grid=(BLOCKS,),
        in_specs=[
            pl.BlockSpec((1, TILE, WIDE), lambda i, s, t: (s[i], 0, 0)),
            pl.BlockSpec((TILE, WIDE), lambda i, s, t: (0, 0)),
        ],
        out_specs=[
            pl.BlockSpec((TILE, HD), lambda i, s, t: (i, 0)),
            pl.BlockSpec((HD + TAIL, TILE), lambda i, s, t: (0, i)),
        ],
    )
    return pl.pallas_call(
        pair_kernel,
        grid_spec=grid_spec,
        out_shape=[
            jax.ShapeDtypeStruct((SEQ, HD), jnp.bfloat16),
            jax.ShapeDtypeStruct((HD + TAIL, SEQ), jnp.bfloat16),
        ],
        compiler_params=params(),
        cost_estimate=cost(SEQ * WIDE, 4 * SEQ * WIDE),
        name="gather_pair",
    )(source, text_at, slots, text)


def attend_kernel(has_base, source, text_at, ends, slots, text, keys, values, *rest):
    out = rest[-1]
    block = pl.program_id(0)
    queries = jnp.where(block == text_at[0], text[...], slots[0])
    queries = jnp.concatenate([queries[:, :HD], queries[:, HD:]], axis=0)
    score_scale = 1.0 / (math.sqrt(HD) * math.log(2.0))
    first = block * TILE
    index = lax.broadcasted_iota(jnp.int32, (1, 2 * TILE), 1)
    position = first + jnp.where(index >= TILE, index - TILE, index)
    start = jnp.zeros_like(position)
    low = jnp.int32(0)
    for at in range(4):
        end = ends[at]
        start = jnp.where(position >= end, end, start)
        low = jnp.where(first >= end, end, low)
    row = lax.broadcasted_iota(jnp.int32, (TILE, 2 * TILE), 0)

    def scores_of(at):
        offset = pl.multiple_of(at * TILE, TILE)
        return lax.dot_general(
            keys[pl.ds(offset, TILE), :],
            queries,
            (((1,), (1,)), ((), ())),
            preferred_element_type=jnp.float32,
        )

    def mix(scores, top, at):
        weights = jnp.exp2((scores - top) * score_scale).astype(jnp.bfloat16)
        offset = pl.multiple_of(at * TILE, TILE)
        return jnp.dot(
            values[:, pl.ds(offset, TILE)], weights, preferred_element_type=jnp.float32
        )

    allowed = (row <= position - first) & (row >= start - first)
    scores = jnp.where(allowed, scores_of(block), masked_score)
    top = jnp.max(scores, axis=0, keepdims=True)
    mixed = mix(scores, top, block)

    def body(at, carry):
        top, mixed = carry
        scores = jnp.where(row >= start - at * TILE, scores_of(at), masked_score)
        higher = jnp.maximum(top, jnp.max(scores, axis=0, keepdims=True))
        fade = jnp.exp2((top - higher) * score_scale)
        return higher, mixed * fade + mix(scores, higher, at)

    top, mixed = lax.fori_loop(low // TILE, block, body, (top, mixed))
    result = (mixed[:HD] / mixed[HD : HD + 1]).T.astype(jnp.bfloat16)
    out[:, :HD] = result[:TILE]
    out[:, HD:] = result[TILE:]


def attend(source, text_at, ends, slots, text, keys, values, base, half, column):
    in_specs = [
        pl.BlockSpec((1, TILE, WIDE), lambda i, s, t, e: (s[i], 0, column)),
        pl.BlockSpec((TILE, WIDE), lambda i, s, t, e: (0, column)),
        pl.BlockSpec((SEQ, HD), lambda i, s, t, e: (0, 0)),
        pl.BlockSpec((HD + TAIL, SEQ), lambda i, s, t, e: (0, 0)),
    ]
    operands = [source, text_at, ends, slots, text, keys, values]
    aliases = {}
    if base is not None:
        in_specs.append(pl.BlockSpec(memory_space=pl.ANY))
        operands.append(base)
        aliases = {7: 0}
    grid_spec = pltpu.PrefetchScalarGridSpec(
        num_scalar_prefetch=3,
        grid=(BLOCKS,),
        in_specs=in_specs,
        out_specs=pl.BlockSpec((TILE, WIDE), lambda i, s, t, e: (i, half)),
    )

    def body(*refs):
        attend_kernel(base is not None, *refs)

    return pl.pallas_call(
        body,
        grid_spec=grid_spec,
        out_shape=jax.ShapeDtypeStruct((SEQ, 2 * WIDE), jnp.bfloat16),
        input_output_aliases=aliases,
        compiler_params=params(),
        cost_estimate=cost(4 * SEQ * SEQ * WIDE, 6 * SEQ * WIDE, SEQ * SEQ),
        name="attend",
    )(*operands)


def local(
    text_rows,
    vis_rows,
    q_weight,
    kv_weight,
    q_bias,
    kv_bias,
    norm_gain,
    tile_dest,
    tile_block,
    doc_lens,
):
    width = norm_gain.shape[0]
    shards = lax.axis_size("dp")
    me = lax.axis_index("dp")
    tensor_at = lax.axis_index("tensor")
    x_at, high = tensor_at // 2, tensor_at % 2
    z_at, low, core = me // 4, me // 2 % 2, me % 2
    blocks = tile_block[0]
    text_block = sum(range(BLOCKS)) - jnp.sum(blocks)

    def squares(rows):
        floats = rows.astype(jnp.float32)
        return jnp.sum(floats * floats, axis=1)

    text_own = lax.dynamic_slice_in_dim(text_rows, text_block * TILE, TILE, 0)
    spread = jnp.concatenate([squares(vis_rows), squares(text_own)]).reshape(BLOCKS, TILE)

    def share(value, bits):
        return jnp.concatenate([value, swap_dp(value, bits)], axis=0)

    def piece(step):
        rows = lax.dynamic_index_in_dim(pieces, (x_at + step) % 4, 0, keepdims=False)
        rows = lax.dynamic_index_in_dim(rows, core, 1, keepdims=False)
        first = lax.dynamic_index_in_dim(rows, high, 0, keepdims=False)
        second = lax.dynamic_index_in_dim(rows, 1 - high, 0, keepdims=False)
        return jnp.concatenate([first, second], axis=0)

    others = [swap_tensor(vis_rows[: 2 * TILE], 1)]
    q_here = mirror_z(q_weight)
    spread = spread + swap_tensor(spread, 2)
    gathered = share(share(tile_block, 2), 1)
    pieces = kv_weight.reshape(4, 2, 2, CORE_PART, WIDE)
    kv_pieces = [piece(step) for step in range(4)]

    q_here, spread, gathered, rows, *kv_pieces = lock(
        (q_here, spread, gathered, vis_rows, *kv_pieces), others
    )
    others.append(swap_tensor(rows[2 * TILE : 4 * TILE], 1))
    q_here = slide_x(q_here)
    spread = spread + swap_tensor(spread, 4)
    kv_third, kv_first = shift_x(kv_pieces[1], 1), shift_x(kv_pieces[3], 3)

    tables = rope_tables(SEQ, HD)
    q_here, spread, gathered, rows, kv_far, kv_first, kv_third, *tables = lock(
        (q_here, spread, gathered, vis_rows, kv_pieces[2], kv_first, kv_third, *tables), others
    )
    q_low = swap_dp(q_here, 2)
    others.append(swap_tensor(rows[4 * TILE : 5 * TILE], 1))
    spread = spread + swap_tensor(spread, 1)
    kv_second = shift_x(kv_far, 2)
    gathered = share(share(gathered, 4), 8)
    last = jnp.concatenate([rows[5 * TILE :], text_own], axis=0)

    own_half = low == high
    q_pair = jnp.concatenate(
        [jnp.where(own_half, q_here, q_low), jnp.where(own_half, q_low, q_here)], axis=0
    )
    q_pair, last, spread, *kv_pieces = lock(
        (q_pair, last, spread, kv_pieces[0], kv_first, kv_second, kv_third), others
    )
    other_last = swap_tensor(last, 1)
    q_pairs = [q_pair[:, :WIDE], q_pair[:, WIDE:]]

    def over_z(pair):
        return [pair] + [shift_z(pair, step) for step in range(1, 4)]

    q_blocks = over_z(q_pairs[0])
    kv_mine = jnp.stack(kv_pieces)
    kv_theirs = swap_dp(kv_mine, 1)

    scale = lax.rsqrt(spread / width + eps).reshape(SEQ, 1)
    gains = norm_gain.reshape(8, 1, PART)
    gain_own = lax.dynamic_index_in_dim(gains, tensor_at, 0, keepdims=False)
    gain_other = lax.dynamic_index_in_dim(gains, tensor_at ^ 1, 0, keepdims=False)
    own = norm_rows(
        jnp.stack([text_block, core]), (vis_rows, text_rows), ((0, 6), (6, 7)), scale, gain_own
    )
    plain = jnp.stack([jnp.int32(0), core])
    other = norm_rows(
        plain, (*others, other_last), ((0, 2), (2, 4), (4, 5), (5, 7)), scale, gain_other
    )

    held = lock((other, own, kv_theirs, q_pairs[1], *q_blocks), ())
    other, own, kv_theirs, q_late = held[:4]
    q_mine = jnp.stack(held[4:])
    q_theirs = swap_dp(q_mine, 1)
    order = [0]
    for bits in (2, 1, 4, 8):
        order = order + [entry ^ bits for entry in order]

    owner_ids = jnp.arange(shards, dtype=jnp.int32)
    source_of = jnp.sum(jnp.where(tile_dest == me, owner_ids[:, None], 0), axis=0)
    my_dest = lax.dynamic_slice_in_dim(tile_dest, me, 1, 0)[0]
    sent = (me ^ jnp.array(order, jnp.int32))[:, None] == my_dest[None, :]
    spots = jnp.concatenate([jnp.sum(jnp.where(sent, gathered, 0), axis=0), text_block[None]])
    dest = jnp.concatenate([my_dest, my_dest[-1:]])
    at_block = blocks[None, :] == jnp.arange(BLOCKS, dtype=jnp.int32)[:, None]
    source = jnp.sum(jnp.where(at_block, source_of[None, :], 0), axis=1)
    text_at = text_block[None]
    ends = jnp.cumsum(doc_lens[0])

    weights = [(kv_mine, kv_theirs, 0), (q_mine, q_theirs, 0)]
    token = []

    def parts(chunk, turns):
        at = []
        for turn in turns:
            group = jnp.where(core == 0, (4 - turn) % 4, turn)
            at.append(group if chunk == 0 else (z_at - group) % 4)
        dtypes = [jnp.bfloat16 if turn else jnp.float32 for turn in turns]
        at = jnp.stack(at).astype(jnp.int32)
        outs = parts_of(at, own, other, *weights[chunk], dtypes, token)
        token[:] = outs[:1]
        return list(outs)

    sums = [parts(0, (1,)), parts(1, (1,))]
    (q_late,) = lock((q_late,), sums[1])
    q_blocks = over_z(q_late)
    sums[0] += parts(0, (2, 3, 0))

    arrived, done = {}, []
    for chunk, turn in [(0, 1), (1, 1), (0, 2), (1, 2), (0, 3), (1, 3), (2, 1), (2, 2), (2, 3)]:
        if (chunk, turn) == (1, 2):
            token[:] = [rows]
            sums[1] += parts(1, (2, 3, 0))
            q_mine = jnp.stack(lock(q_blocks, sums[1][3:]))
            weights.append((q_mine, swap_dp(q_mine, 1), 0))
            sums.append(parts(2, (1, 2, 3, 0)))
        if (chunk, turn) == (2, 1):
            (arrived[0],) = lock((arrived[0],), sums[2][:1])
        rows = sums[chunk][turn - 1]
        guards = done[-2:-1]
        if turn > 1:
            rows, got = lock((rows, arrived[chunk]), guards)
            rows = (rows.astype(jnp.float32) + got.astype(jnp.float32)).astype(jnp.bfloat16)
        elif guards:
            (rows,) = lock((rows,), guards)
        arrived[chunk] = ring_x(rows)
        done.append(arrived[chunk])

    biases = [kv_bias.reshape(1, WIDE), q_bias[None, :WIDE], q_bias[None, WIDE:]]
    routed = []
    for chunks, rotated in (((0, 1), (1, 0, 1, 1)), ((2,), (1, 1))):
        slots, text = finish(
            rotated,
            dest,
            spots,
            [sums[chunk][3] for chunk in chunks],
            [arrived[chunk] for chunk in chunks],
            [biases[chunk] for chunk in chunks],
            tables,
            shards,
        )
        filled = lax.all_to_all(slots, "dp", split_axis=0, concat_axis=0, tiled=True)
        routed.append((filled, text))
    pair = gather_pair(source, text_at, *routed[0])
    context = attend(source, text_at, ends, *routed[0], *pair, None, 0, 1)
    return attend(source, text_at, ends, *routed[1], *pair, context, 1, 0)


def solution(mesh):
    in_specs = (
        P("dp", "tensor"),
        P("dp", "tensor"),
        P("dp", "tensor"),
        P(None, None, "tensor"),
        P("tensor"),
        P(None, "tensor"),
        P(),
        P(),
        P("dp", None),
        P("dp", None),
    )
    out_specs = P("dp", "tensor")
    return jax.shard_map(local, mesh=mesh, in_specs=in_specs, out_specs=out_specs, check_vma=False)
```

```python
import functools
import math

import jax
import jax.numpy as jnp
from jax import lax
from jax.experimental import pallas as pl
from jax.experimental.pallas import tpu as pltpu
from jax.sharding import PartitionSpec as P

HD = 128
TILE = 256
BLOCKS = 7
SEQ = BLOCKS * TILE
PART = 1024
SLICE = 2 * PART
CORE_PART = PART // 2
TAIL = 16
WIDE = 2 * HD
ROWS = SEQ // 4
VMEM = 48 * 1024 * 1024

rope_base = 1000000.0
eps = 1e-06
masked_score = -1e30


def params():
    return pltpu.CompilerParams(vmem_limit_bytes=VMEM)


def cost(flops, moved, transcendentals=0):
    return pl.CostEstimate(flops=flops, bytes_accessed=moved, transcendentals=transcendentals)


def rope_tables(length, width):
    half_width = width // 2
    inverse = rope_base ** (-(jnp.arange(half_width, dtype=jnp.float32) * 2.0) / width)
    angles = jnp.arange(length, dtype=jnp.float32)[:, None] * inverse[None, :]
    cosine, sine = jnp.cos(angles), jnp.sin(angles)
    return (
        jnp.concatenate([cosine, cosine], axis=1),
        jnp.concatenate([-sine, sine], axis=1),
    )


def shift_x(value, step):
    pairs = [
        (2 * x + high, 2 * ((x + step) % 4) + high) for x in range(4) for high in range(2)
    ]
    return lax.ppermute(value, "tensor", pairs)


def swap_tensor(value, bits):
    return lax.ppermute(value, "tensor", [(t, t ^ bits) for t in range(8)])


def swap_dp(value, bits):
    return lax.ppermute(value, "dp", [(d, d ^ bits) for d in range(16)])


def place(z, low, core, x, high):
    return ((z * 2 + low) * 2 + core) * 8 + x * 2 + high


def all_places():
    return [
        (z, low, core, x, high)
        for z in range(4)
        for low in range(2)
        for core in range(2)
        for x in range(4)
        for high in range(2)
    ]


def ring_x(value):
    pairs = [
        (place(z, low, core, x, high), place(z, low, core, (x + 1 - 2 * core) % 4, high))
        for z, low, core, x, high in all_places()
    ]
    return lax.ppermute(value, ("dp", "tensor"), pairs)


def shift_z(value, step):
    return lax.ppermute(value, "dp", [(d, (d + 4 * step) % 16) for d in range(16)])


def mirror_z(value):
    pairs = [
        (place(z, low, core, x, high), place((x - z) % 4, low, core, x, high))
        for z, low, core, x, high in all_places()
    ]
    return lax.ppermute(value, ("dp", "tensor"), pairs)


def slide_x(value):
    pairs = [
        (place(z, low, core, x, high), place(z, low, core, (x - z) % 4, high))
        for z, low, core, x, high in all_places()
    ]
    return lax.ppermute(value, ("dp", "tensor"), pairs)


def lock(values, guards):
    return lax.optimization_barrier((tuple(values), tuple(guards)))[0]


def norm_kernel(bounds, begin, picks, *refs):
    parts, scale, gain, out = refs[: len(bounds)], refs[len(bounds)], refs[len(bounds) + 1], refs[-1]
    step = pl.program_id(0) + begin
    core = picks[1]

    def put(rows):
        result = (rows[...].astype(jnp.float32) * scale[...] * gain[...]).astype(jnp.bfloat16)
        front, back = result[:, :CORE_PART], result[:, CORE_PART:]

        @pl.when(core == 0)
        def _():
            out[:, :CORE_PART] = front
            out[:, CORE_PART:] = back

        @pl.when(core == 1)
        def _():
            out[:, :CORE_PART] = back
            out[:, CORE_PART:] = front

    for part, (first, last) in zip(parts, bounds):
        pl.when((step >= first) & (step < last))(functools.partial(put, part))


def norm_rows(picks, parts, bounds, scale, gain, base=None):
    begin, end = bounds[0][0], bounds[-1][1]

    def spec(part, first, last):
        if part.shape[0] == SEQ:
            return pl.BlockSpec((TILE, PART), lambda i, s: (s[0], 0))
        return pl.BlockSpec(
            (TILE, PART), lambda i, s: (jnp.clip(i + begin - first, 0, last - first - 1), 0)
        )

    aliased = [] if base is None else [base]
    grid_spec = pltpu.PrefetchScalarGridSpec(
        num_scalar_prefetch=1,
        grid=(end - begin,),
        in_specs=[spec(part, *bound) for part, bound in zip(parts, bounds)]
        + [
            pl.BlockSpec((TILE, 1), lambda i, s: (i + begin, 0)),
            pl.BlockSpec((1, PART), lambda i, s: (0, 0)),
        ]
        + later(aliased),
        out_specs=pl.BlockSpec((TILE, PART), lambda i, s: (i + begin, 0)),
    )
    rows = (end - begin) * TILE
    return pl.pallas_call(
        functools.partial(norm_kernel, bounds, begin),
        grid_spec=grid_spec,
        out_shape=jax.ShapeDtypeStruct((SEQ, PART), jnp.bfloat16),
        input_output_aliases={len(parts) + 3: 0} if aliased else {},
        compiler_params=params(),
        cost_estimate=cost(0, 0),
        name="norm_rows",
    )(picks, *parts, scale, gain, *aliased)


def later(tokens):
    return [pl.BlockSpec(memory_space=pl.ANY)] * len(tokens)


def part_kernel(count, at, own, other, *rest):
    weights, outs = rest[: 2 * count], rest[-count:]
    for turn in range(count):
        total = None
        for columns, part in zip(
            (slice(0, CORE_PART), slice(CORE_PART, PART)), weights[2 * turn : 2 * turn + 2]
        ):
            for rows, at in ((own, slice(0, CORE_PART)), (other, slice(CORE_PART, PART))):
                term = jnp.dot(rows[:, columns], part[0, at], preferred_element_type=jnp.float32)
                total = term if total is None else total + term
        outs[turn][...] = total.astype(outs[turn].dtype)


def parts_of(at, own, other, mine, theirs, half, dtypes, tokens):
    count = len(dtypes)

    def weight_spec(turn):
        return pl.BlockSpec((1, PART, WIDE), lambda i, s: (s[turn], 0, half))

    grid_spec = pltpu.PrefetchScalarGridSpec(
        num_scalar_prefetch=1,
        grid=(SEQ // ROWS,),
        in_specs=[
            pl.BlockSpec((ROWS, PART), lambda i, s: (i, 0)),
            pl.BlockSpec((ROWS, PART), lambda i, s: (i, 0)),
            *[weight_spec(turn) for turn in range(count) for _ in range(2)],
            *later(tokens),
        ],
        out_specs=[pl.BlockSpec((ROWS, WIDE), lambda i, s: (i, 0))] * count,
    )
    return pl.pallas_call(
        functools.partial(part_kernel, count),
        grid_spec=grid_spec,
        out_shape=[jax.ShapeDtypeStruct((SEQ, WIDE), dtype) for dtype in dtypes],
        compiler_params=params(),
        cost_estimate=cost(2 * count * SEQ * SLICE * WIDE, 2 * SEQ * SLICE),
        name="part_rows",
    )(at, own, other, *[mine, theirs] * count, *tokens)


def finish_kernel(rotated, dest, spots, *refs):
    count = len(rotated) // 2
    heres, gots, biases = refs[:count], refs[count : 2 * count], refs[2 * count : 3 * count]
    cosine, sine, slots, text = refs[3 * count :]
    step = pl.program_id(0)
    heads = []
    for at in range(count):
        total = heres[at][...] + gots[at][...].astype(jnp.float32) + biases[at][...]
        for head in range(2):
            values = total[:, head * HD : (head + 1) * HD]
            if rotated[2 * at + head]:
                values = values * cosine[...] + pltpu.roll(values, HD // 2, 1) * sine[...]
            heads.append(values.astype(jnp.bfloat16))

    @pl.when(step < BLOCKS - 1)
    def _():
        for head, values in enumerate(heads):
            slots[0, :, head * HD : (head + 1) * HD] = values

    @pl.when(step == BLOCKS - 1)
    def _():
        for head, values in enumerate(heads):
            text[:, head * HD : (head + 1) * HD] = values


def finish(rotated, dest, spots, heres, gots, biases, tables, shards):
    count = len(heres)

    def row(i, d, s):
        return (i, 0)

    def spot(i, d, s):
        return (s[i], 0)

    def none(i, d, s):
        return (0, 0)

    grid_spec = pltpu.PrefetchScalarGridSpec(
        num_scalar_prefetch=2,
        grid=(BLOCKS,),
        in_specs=[
            *[pl.BlockSpec((TILE, WIDE), row)] * (2 * count),
            *[pl.BlockSpec((1, WIDE), none)] * count,
            pl.BlockSpec((TILE, HD), spot),
            pl.BlockSpec((TILE, HD), spot),
        ],
        out_specs=[
            pl.BlockSpec((1, TILE, count * WIDE), lambda i, d, s: (d[i], 0, 0)),
            pl.BlockSpec((TILE, count * WIDE), none),
        ],
    )
    return pl.pallas_call(
        functools.partial(finish_kernel, rotated),
        grid_spec=grid_spec,
        out_shape=[
            jax.ShapeDtypeStruct((shards, TILE, count * WIDE), jnp.bfloat16),
            jax.ShapeDtypeStruct((TILE, count * WIDE), jnp.bfloat16),
        ],
        compiler_params=params(),
        cost_estimate=cost(8 * count * SEQ * WIDE, 10 * count * SEQ * WIDE),
        name="finish_rows",
    )(dest, spots, *heres, *gots, *biases, *tables)


def pair_kernel(source, text_at, slots, text, keys, values):
    block = pl.program_id(0)

    def put(rows):
        keys[...] = rows[:, :HD]
        values[:HD] = rows[:, HD:].T
        values[HD:] = jnp.ones((TAIL, TILE), jnp.bfloat16)

    @pl.when(text_at[0] == block)
    def _():
        put(text[...])

    @pl.when(text_at[0] != block)
    def _():
        put(slots[0])


def gather_pair(source, text_at, slots, text):
    grid_spec = pltpu.PrefetchScalarGridSpec(
        num_scalar_prefetch=2,
        grid=(BLOCKS,),
        in_specs=[
            pl.BlockSpec((1, TILE, WIDE), lambda i, s, t: (s[i], 0, 0)),
            pl.BlockSpec((TILE, WIDE), lambda i, s, t: (0, 0)),
        ],
        out_specs=[
            pl.BlockSpec((TILE, HD), lambda i, s, t: (i, 0)),
            pl.BlockSpec((HD + TAIL, TILE), lambda i, s, t: (0, i)),
        ],
    )
    return pl.pallas_call(
        pair_kernel,
        grid_spec=grid_spec,
        out_shape=[
            jax.ShapeDtypeStruct((SEQ, HD), jnp.bfloat16),
            jax.ShapeDtypeStruct((HD + TAIL, SEQ), jnp.bfloat16),
        ],
        compiler_params=params(),
        cost_estimate=cost(SEQ * WIDE, 4 * SEQ * WIDE),
        name="gather_pair",
    )(source, text_at, slots, text)


def attend_kernel(has_base, source, text_at, ends, slots, text, keys, values, *rest):
    out = rest[-1]
    block = pl.program_id(0)
    queries = jnp.where(block == text_at[0], text[...], slots[0])
    queries = jnp.concatenate([queries[:, :HD], queries[:, HD:]], axis=0)
    score_scale = 1.0 / (math.sqrt(HD) * math.log(2.0))
    first = block * TILE
    index = lax.broadcasted_iota(jnp.int32, (1, 2 * TILE), 1)
    position = first + jnp.where(index >= TILE, index - TILE, index)
    start = jnp.zeros_like(position)
    low = jnp.int32(0)
    for at in range(4):
        end = ends[at]
        start = jnp.where(position >= end, end, start)
        low = jnp.where(first >= end, end, low)
    row = lax.broadcasted_iota(jnp.int32, (TILE, 2 * TILE), 0)

    def scores_of(at):
        offset = pl.multiple_of(at * TILE, TILE)
        return lax.dot_general(
            keys[pl.ds(offset, TILE), :],
            queries,
            (((1,), (1,)), ((), ())),
            preferred_element_type=jnp.float32,
        )

    def mix(scores, top, at):
        weights = jnp.exp2((scores - top) * score_scale).astype(jnp.bfloat16)
        offset = pl.multiple_of(at * TILE, TILE)
        return jnp.dot(
            values[:, pl.ds(offset, TILE)], weights, preferred_element_type=jnp.float32
        )

    allowed = (row <= position - first) & (row >= start - first)
    scores = jnp.where(allowed, scores_of(block), masked_score)
    top = jnp.max(scores, axis=0, keepdims=True)
    mixed = mix(scores, top, block)

    def body(at, carry):
        top, mixed = carry
        scores = jnp.where(row >= start - at * TILE, scores_of(at), masked_score)
        higher = jnp.maximum(top, jnp.max(scores, axis=0, keepdims=True))
        fade = jnp.exp2((top - higher) * score_scale)
        return higher, mixed * fade + mix(scores, higher, at)

    top, mixed = lax.fori_loop(low // TILE, block, body, (top, mixed))
    result = (mixed[:HD] / mixed[HD : HD + 1]).T.astype(jnp.bfloat16)
    out[:, :HD] = result[:TILE]
    out[:, HD:] = result[TILE:]


def attend(source, text_at, ends, slots, text, keys, values, base, half, column):
    in_specs = [
        pl.BlockSpec((1, TILE, WIDE), lambda i, s, t, e: (s[i], 0, column)),
        pl.BlockSpec((TILE, WIDE), lambda i, s, t, e: (0, column)),
        pl.BlockSpec((SEQ, HD), lambda i, s, t, e: (0, 0)),
        pl.BlockSpec((HD + TAIL, SEQ), lambda i, s, t, e: (0, 0)),
    ]
    operands = [source, text_at, ends, slots, text, keys, values]
    aliases = {}
    if base is not None:
        in_specs.append(pl.BlockSpec(memory_space=pl.ANY))
        operands.append(base)
        aliases = {7: 0}
    grid_spec = pltpu.PrefetchScalarGridSpec(
        num_scalar_prefetch=3,
        grid=(BLOCKS,),
        in_specs=in_specs,
        out_specs=pl.BlockSpec((TILE, WIDE), lambda i, s, t, e: (i, half)),
    )

    def body(*refs):
        attend_kernel(base is not None, *refs)

    return pl.pallas_call(
        body,
        grid_spec=grid_spec,
        out_shape=jax.ShapeDtypeStruct((SEQ, 2 * WIDE), jnp.bfloat16),
        input_output_aliases=aliases,
        compiler_params=params(),
        cost_estimate=cost(4 * SEQ * SEQ * WIDE, 6 * SEQ * WIDE, SEQ * SEQ),
        name="attend",
    )(*operands)


def local(
    text_rows,
    vis_rows,
    q_weight,
    kv_weight,
    q_bias,
    kv_bias,
    norm_gain,
    tile_dest,
    tile_block,
    doc_lens,
):
    width = norm_gain.shape[0]
    shards = lax.axis_size("dp")
    me = lax.axis_index("dp")
    tensor_at = lax.axis_index("tensor")
    x_at, high = tensor_at // 2, tensor_at % 2
    z_at, low, core = me // 4, me // 2 % 2, me % 2
    blocks = tile_block[0]
    text_block = sum(range(BLOCKS)) - jnp.sum(blocks)

    def squares(rows):
        floats = rows.astype(jnp.float32)
        return jnp.sum(floats * floats, axis=1)

    text_own = lax.dynamic_slice_in_dim(text_rows, text_block * TILE, TILE, 0)
    spread = jnp.concatenate([squares(vis_rows), squares(text_own)]).reshape(BLOCKS, TILE)

    def share(value, bits):
        return jnp.concatenate([value, swap_dp(value, bits)], axis=0)

    def piece(step):
        rows = lax.dynamic_index_in_dim(pieces, (x_at + step) % 4, 0, keepdims=False)
        rows = lax.dynamic_index_in_dim(rows, core, 1, keepdims=False)
        first = lax.dynamic_index_in_dim(rows, high, 0, keepdims=False)
        second = lax.dynamic_index_in_dim(rows, 1 - high, 0, keepdims=False)
        return jnp.concatenate([first, second], axis=0)

    others = [swap_tensor(vis_rows[: 2 * TILE], 1)]
    q_here = mirror_z(q_weight)
    spread = spread + swap_tensor(spread, 2)
    gathered = share(share(tile_block, 2), 1)
    pieces = kv_weight.reshape(4, 2, 2, CORE_PART, WIDE)
    kv_pieces = [piece(step) for step in range(4)]

    q_here, spread, gathered, rows, *kv_pieces = lock(
        (q_here, spread, gathered, vis_rows, *kv_pieces), others
    )
    others.append(swap_tensor(rows[2 * TILE : 4 * TILE], 1))
    q_here = slide_x(q_here)
    spread = spread + swap_tensor(spread, 4)
    kv_third, kv_first = shift_x(kv_pieces[1], 1), shift_x(kv_pieces[3], 3)

    tables = rope_tables(SEQ, HD)
    q_here, spread, gathered, rows, kv_far, kv_first, kv_third, *tables = lock(
        (q_here, spread, gathered, vis_rows, kv_pieces[2], kv_first, kv_third, *tables), others
    )
    q_low = swap_dp(q_here, 2)
    others.append(swap_tensor(rows[4 * TILE : 5 * TILE], 1))
    spread = spread + swap_tensor(spread, 1)
    kv_second = shift_x(kv_far, 2)
    gathered = share(share(gathered, 4), 8)
    last = jnp.concatenate([rows[5 * TILE :], text_own], axis=0)

    own_half = low == high
    q_pair = jnp.concatenate(
        [jnp.where(own_half, q_here, q_low), jnp.where(own_half, q_low, q_here)], axis=0
    )
    q_pair, last, spread, *kv_pieces = lock(
        (q_pair, last, spread, kv_pieces[0], kv_first, kv_second, kv_third), others
    )
    other_last = swap_tensor(last, 1)
    q_pairs = [q_pair[:, :WIDE], q_pair[:, WIDE:]]

    def over_z(pair):
        return [pair] + [shift_z(pair, step) for step in range(1, 4)]

    q_blocks = over_z(q_pairs[0])
    kv_mine = jnp.stack(kv_pieces)
    kv_theirs = swap_dp(kv_mine, 1)

    scale = lax.rsqrt(spread / width + eps).reshape(SEQ, 1)
    gains = norm_gain.reshape(8, 1, PART)
    gain_own = lax.dynamic_index_in_dim(gains, tensor_at, 0, keepdims=False)
    gain_other = lax.dynamic_index_in_dim(gains, tensor_at ^ 1, 0, keepdims=False)
    own = norm_rows(
        jnp.stack([text_block, core]), (vis_rows, text_rows), ((0, 6), (6, 7)), scale, gain_own
    )
    plain = jnp.stack([jnp.int32(0), core])
    other = norm_rows(
        plain, (*others, other_last), ((0, 2), (2, 4), (4, 5), (5, 7)), scale, gain_other
    )

    held = lock((other, own, kv_theirs, q_pairs[1], gathered, *q_blocks), ())
    other, own, kv_theirs, q_late, gathered = held[:5]
    q_mine = jnp.stack(held[5:])
    q_theirs = swap_dp(q_mine, 1)
    order = [0]
    for bits in (2, 1, 4, 8):
        order = order + [entry ^ bits for entry in order]

    owner_ids = jnp.arange(shards, dtype=jnp.int32)
    source_of = jnp.sum(jnp.where(tile_dest == me, owner_ids[:, None], 0), axis=0)
    my_dest = lax.dynamic_slice_in_dim(tile_dest, me, 1, 0)[0]
    sent = (me ^ jnp.array(order, jnp.int32))[:, None] == my_dest[None, :]
    spots = jnp.concatenate([jnp.sum(jnp.where(sent, gathered, 0), axis=0), text_block[None]])
    dest = jnp.concatenate([my_dest, my_dest[-1:]])
    at_block = blocks[None, :] == jnp.arange(BLOCKS, dtype=jnp.int32)[:, None]
    source = jnp.sum(jnp.where(at_block, source_of[None, :], 0), axis=1)
    text_at = text_block[None]
    ends = jnp.cumsum(doc_lens[0])

    weights = [(kv_mine, kv_theirs, 0), (q_mine, q_theirs, 0)]
    token = []

    def parts(chunk, turns):
        at = []
        for turn in turns:
            group = jnp.where(core == 0, (4 - turn) % 4, turn)
            at.append(group if chunk == 0 else (z_at - group) % 4)
        dtypes = [jnp.bfloat16 if turn else jnp.float32 for turn in turns]
        at = jnp.stack(at).astype(jnp.int32)
        outs = parts_of(at, own, other, *weights[chunk], dtypes, token)
        token[:] = outs[:1]
        return list(outs)

    sums = [parts(0, (1,)), parts(1, (1,))]
    (q_late,) = lock((q_late,), sums[1])
    q_blocks = over_z(q_late)
    sums[0] += parts(0, (2, 3, 0))

    arrived, done = {}, []
    for chunk, turn in [(0, 1), (1, 1), (0, 2), (1, 2), (0, 3), (1, 3), (2, 1), (2, 2), (2, 3)]:
        if (chunk, turn) == (1, 2):
            token[:] = [rows]
            sums[1] += parts(1, (2, 3, 0))
            q_mine = jnp.stack(lock(q_blocks, sums[1][3:]))
            weights.append((q_mine, swap_dp(q_mine, 1), 0))
            sums.append(parts(2, (1, 2, 3, 0)))
        if (chunk, turn) == (2, 1):
            (arrived[0],) = lock((arrived[0],), sums[2][:1])
        rows = sums[chunk][turn - 1]
        guards = done[-2:-1]
        if turn > 1:
            rows, got = lock((rows, arrived[chunk]), guards)
            rows = (rows.astype(jnp.float32) + got.astype(jnp.float32)).astype(jnp.bfloat16)
        elif guards:
            (rows,) = lock((rows,), guards)
        arrived[chunk] = ring_x(rows)
        done.append(arrived[chunk])

    biases = [kv_bias.reshape(1, WIDE), q_bias[None, :WIDE], q_bias[None, WIDE:]]
    routed = []
    for chunks, rotated in (((0, 1), (1, 0, 1, 1)), ((2,), (1, 1))):
        slots, text = finish(
            rotated,
            dest,
            spots,
            [sums[chunk][3] for chunk in chunks],
            [arrived[chunk] for chunk in chunks],
            [biases[chunk] for chunk in chunks],
            tables,
            shards,
        )
        filled = lax.all_to_all(slots, "dp", split_axis=0, concat_axis=0, tiled=True)
        routed.append((filled, text))
    pair = gather_pair(source, text_at, *routed[0])
    context = attend(source, text_at, ends, *routed[0], *pair, None, 0, 1)
    return attend(source, text_at, ends, *routed[1], *pair, context, 1, 0)


def solution(mesh):
    in_specs = (
        P("dp", "tensor"),
        P("dp", "tensor"),
        P("dp", "tensor"),
        P(None, None, "tensor"),
        P("tensor"),
        P(None, "tensor"),
        P(),
        P(),
        P("dp", None),
        P("dp", None),
    )
    out_specs = P("dp", "tensor")
    return jax.shard_map(local, mesh=mesh, in_specs=in_specs, out_specs=out_specs, check_vma=False)
```

```python
import functools
import math

import jax
import jax.numpy as jnp
from jax import lax
from jax.experimental import pallas as pl
from jax.experimental.pallas import tpu as pltpu
from jax.sharding import PartitionSpec as P

HD = 128
TILE = 256
BLOCKS = 7
SEQ = BLOCKS * TILE
PART = 1024
SLICE = 2 * PART
CORE_PART = PART // 2
TAIL = 16
WIDE = 2 * HD
ROWS = SEQ // 4
VMEM = 48 * 1024 * 1024

rope_base = 1000000.0
eps = 1e-06
masked_score = -1e30


def params():
    return pltpu.CompilerParams(vmem_limit_bytes=VMEM)


def cost(flops, moved, transcendentals=0):
    return pl.CostEstimate(flops=flops, bytes_accessed=moved, transcendentals=transcendentals)


def rope_tables(length, width):
    half_width = width // 2
    inverse = rope_base ** (-(jnp.arange(half_width, dtype=jnp.float32) * 2.0) / width)
    angles = jnp.arange(length, dtype=jnp.float32)[:, None] * inverse[None, :]
    cosine, sine = jnp.cos(angles), jnp.sin(angles)
    return (
        jnp.concatenate([cosine, cosine], axis=1),
        jnp.concatenate([-sine, sine], axis=1),
    )


def shift_x(value, step):
    pairs = [
        (2 * x + high, 2 * ((x + step) % 4) + high) for x in range(4) for high in range(2)
    ]
    return lax.ppermute(value, "tensor", pairs)


def swap_tensor(value, bits):
    return lax.ppermute(value, "tensor", [(t, t ^ bits) for t in range(8)])


def swap_dp(value, bits):
    return lax.ppermute(value, "dp", [(d, d ^ bits) for d in range(16)])


def place(z, low, core, x, high):
    return ((z * 2 + low) * 2 + core) * 8 + x * 2 + high


def all_places():
    return [
        (z, low, core, x, high)
        for z in range(4)
        for low in range(2)
        for core in range(2)
        for x in range(4)
        for high in range(2)
    ]


def ring_x(value):
    pairs = [
        (place(z, low, core, x, high), place(z, low, core, (x + 1 - 2 * core) % 4, high))
        for z, low, core, x, high in all_places()
    ]
    return lax.ppermute(value, ("dp", "tensor"), pairs)


def shift_z(value, step):
    return lax.ppermute(value, "dp", [(d, (d + 4 * step) % 16) for d in range(16)])


def mirror_z(value):
    pairs = [
        (place(z, low, core, x, high), place((x - z) % 4, low, core, x, high))
        for z, low, core, x, high in all_places()
    ]
    return lax.ppermute(value, ("dp", "tensor"), pairs)


def slide_x(value):
    pairs = [
        (place(z, low, core, x, high), place(z, low, core, (x - z) % 4, high))
        for z, low, core, x, high in all_places()
    ]
    return lax.ppermute(value, ("dp", "tensor"), pairs)


def lock(values, guards):
    return lax.optimization_barrier((tuple(values), tuple(guards)))[0]


def norm_kernel(bounds, begin, picks, *refs):
    parts, scale, gain, out = refs[: len(bounds)], refs[len(bounds)], refs[len(bounds) + 1], refs[-1]
    step = pl.program_id(0) + begin
    core = picks[1]

    def put(rows):
        result = (rows[...].astype(jnp.float32) * scale[...] * gain[...]).astype(jnp.bfloat16)
        front, back = result[:, :CORE_PART], result[:, CORE_PART:]

        @pl.when(core == 0)
        def _():
            out[:, :CORE_PART] = front
            out[:, CORE_PART:] = back

        @pl.when(core == 1)
        def _():
            out[:, :CORE_PART] = back
            out[:, CORE_PART:] = front

    for part, (first, last) in zip(parts, bounds):
        pl.when((step >= first) & (step < last))(functools.partial(put, part))


def norm_rows(picks, parts, bounds, scale, gain, base=None):
    begin, end = bounds[0][0], bounds[-1][1]

    def spec(part, first, last):
        if part.shape[0] == SEQ:
            return pl.BlockSpec((TILE, PART), lambda i, s: (s[0], 0))
        return pl.BlockSpec(
            (TILE, PART), lambda i, s: (jnp.clip(i + begin - first, 0, last - first - 1), 0)
        )

    aliased = [] if base is None else [base]
    grid_spec = pltpu.PrefetchScalarGridSpec(
        num_scalar_prefetch=1,
        grid=(end - begin,),
        in_specs=[spec(part, *bound) for part, bound in zip(parts, bounds)]
        + [
            pl.BlockSpec((TILE, 1), lambda i, s: (i + begin, 0)),
            pl.BlockSpec((1, PART), lambda i, s: (0, 0)),
        ]
        + later(aliased),
        out_specs=pl.BlockSpec((TILE, PART), lambda i, s: (i + begin, 0)),
    )
    rows = (end - begin) * TILE
    return pl.pallas_call(
        functools.partial(norm_kernel, bounds, begin),
        grid_spec=grid_spec,
        out_shape=jax.ShapeDtypeStruct((SEQ, PART), jnp.bfloat16),
        input_output_aliases={len(parts) + 3: 0} if aliased else {},
        compiler_params=params(),
        cost_estimate=cost(0, 0),
        name="norm_rows",
    )(picks, *parts, scale, gain, *aliased)


def later(tokens):
    return [pl.BlockSpec(memory_space=pl.ANY)] * len(tokens)


def part_kernel(count, at, own, other, *rest):
    weights, outs = rest[: 2 * count], rest[-count:]
    for turn in range(count):
        total = None
        for columns, part in zip(
            (slice(0, CORE_PART), slice(CORE_PART, PART)), weights[2 * turn : 2 * turn + 2]
        ):
            for rows, at in ((own, slice(0, CORE_PART)), (other, slice(CORE_PART, PART))):
                term = jnp.dot(rows[:, columns], part[0, at], preferred_element_type=jnp.float32)
                total = term if total is None else total + term
        outs[turn][...] = total.astype(outs[turn].dtype)


def parts_of(at, own, other, mine, theirs, half, dtypes, tokens):
    count = len(dtypes)
    rows = 2 * ROWS if count == 1 else ROWS

    def weight_spec(turn):
        return pl.BlockSpec((1, PART, WIDE), lambda i, s: (s[turn], 0, half))

    grid_spec = pltpu.PrefetchScalarGridSpec(
        num_scalar_prefetch=1,
        grid=(SEQ // rows,),
        in_specs=[
            pl.BlockSpec((rows, PART), lambda i, s: (i, 0)),
            pl.BlockSpec((rows, PART), lambda i, s: (i, 0)),
            *[weight_spec(turn) for turn in range(count) for _ in range(2)],
            *later(tokens),
        ],
        out_specs=[pl.BlockSpec((rows, WIDE), lambda i, s: (i, 0))] * count,
    )
    return pl.pallas_call(
        functools.partial(part_kernel, count),
        grid_spec=grid_spec,
        out_shape=[jax.ShapeDtypeStruct((SEQ, WIDE), dtype) for dtype in dtypes],
        compiler_params=params(),
        cost_estimate=cost(2 * count * SEQ * SLICE * WIDE, 2 * SEQ * SLICE),
        name="part_rows",
    )(at, own, other, *[mine, theirs] * count, *tokens)


def finish_kernel(rotated, dest, spots, *refs):
    count = len(rotated) // 2
    heres, gots, biases = refs[:count], refs[count : 2 * count], refs[2 * count : 3 * count]
    cosine, sine, slots, text = refs[3 * count :]
    step = pl.program_id(0)
    heads = []
    for at in range(count):
        total = heres[at][...] + gots[at][...].astype(jnp.float32) + biases[at][...]
        for head in range(2):
            values = total[:, head * HD : (head + 1) * HD]
            if rotated[2 * at + head]:
                values = values * cosine[...] + pltpu.roll(values, HD // 2, 1) * sine[...]
            heads.append(values.astype(jnp.bfloat16))

    @pl.when(step < BLOCKS - 1)
    def _():
        for head, values in enumerate(heads):
            slots[0, :, head * HD : (head + 1) * HD] = values

    @pl.when(step == BLOCKS - 1)
    def _():
        for head, values in enumerate(heads):
            text[:, head * HD : (head + 1) * HD] = values


def finish(rotated, dest, spots, heres, gots, biases, tables, shards):
    count = len(heres)

    def row(i, d, s):
        return (i, 0)

    def spot(i, d, s):
        return (s[i], 0)

    def none(i, d, s):
        return (0, 0)

    grid_spec = pltpu.PrefetchScalarGridSpec(
        num_scalar_prefetch=2,
        grid=(BLOCKS,),
        in_specs=[
            *[pl.BlockSpec((TILE, WIDE), row)] * (2 * count),
            *[pl.BlockSpec((1, WIDE), none)] * count,
            pl.BlockSpec((TILE, HD), spot),
            pl.BlockSpec((TILE, HD), spot),
        ],
        out_specs=[
            pl.BlockSpec((1, TILE, count * WIDE), lambda i, d, s: (d[i], 0, 0)),
            pl.BlockSpec((TILE, count * WIDE), none),
        ],
    )
    return pl.pallas_call(
        functools.partial(finish_kernel, rotated),
        grid_spec=grid_spec,
        out_shape=[
            jax.ShapeDtypeStruct((shards, TILE, count * WIDE), jnp.bfloat16),
            jax.ShapeDtypeStruct((TILE, count * WIDE), jnp.bfloat16),
        ],
        compiler_params=params(),
        cost_estimate=cost(8 * count * SEQ * WIDE, 10 * count * SEQ * WIDE),
        name="finish_rows",
    )(dest, spots, *heres, *gots, *biases, *tables)


def pair_kernel(source, text_at, slots, text, keys, values):
    block = pl.program_id(0)

    def put(rows):
        keys[...] = rows[:, :HD]
        values[:HD] = rows[:, HD:].T
        values[HD:] = jnp.ones((TAIL, TILE), jnp.bfloat16)

    @pl.when(text_at[0] == block)
    def _():
        put(text[...])

    @pl.when(text_at[0] != block)
    def _():
        put(slots[0])


def gather_pair(source, text_at, slots, text):
    grid_spec = pltpu.PrefetchScalarGridSpec(
        num_scalar_prefetch=2,
        grid=(BLOCKS,),
        in_specs=[
            pl.BlockSpec((1, TILE, WIDE), lambda i, s, t: (s[i], 0, 0)),
            pl.BlockSpec((TILE, WIDE), lambda i, s, t: (0, 0)),
        ],
        out_specs=[
            pl.BlockSpec((TILE, HD), lambda i, s, t: (i, 0)),
            pl.BlockSpec((HD + TAIL, TILE), lambda i, s, t: (0, i)),
        ],
    )
    return pl.pallas_call(
        pair_kernel,
        grid_spec=grid_spec,
        out_shape=[
            jax.ShapeDtypeStruct((SEQ, HD), jnp.bfloat16),
            jax.ShapeDtypeStruct((HD + TAIL, SEQ), jnp.bfloat16),
        ],
        compiler_params=params(),
        cost_estimate=cost(SEQ * WIDE, 4 * SEQ * WIDE),
        name="gather_pair",
    )(source, text_at, slots, text)


def attend_kernel(has_base, source, text_at, ends, slots, text, keys, values, *rest):
    out = rest[-1]
    block = pl.program_id(0)
    queries = jnp.where(block == text_at[0], text[...], slots[0])
    queries = jnp.concatenate([queries[:, :HD], queries[:, HD:]], axis=0)
    score_scale = 1.0 / (math.sqrt(HD) * math.log(2.0))
    first = block * TILE
    index = lax.broadcasted_iota(jnp.int32, (1, 2 * TILE), 1)
    position = first + jnp.where(index >= TILE, index - TILE, index)
    start = jnp.zeros_like(position)
    low = jnp.int32(0)
    for at in range(4):
        end = ends[at]
        start = jnp.where(position >= end, end, start)
        low = jnp.where(first >= end, end, low)
    row = lax.broadcasted_iota(jnp.int32, (TILE, 2 * TILE), 0)

    def scores_of(at):
        offset = pl.multiple_of(at * TILE, TILE)
        return lax.dot_general(
            keys[pl.ds(offset, TILE), :],
            queries,
            (((1,), (1,)), ((), ())),
            preferred_element_type=jnp.float32,
        )

    def mix(scores, top, at):
        weights = jnp.exp2((scores - top) * score_scale).astype(jnp.bfloat16)
        offset = pl.multiple_of(at * TILE, TILE)
        return jnp.dot(
            values[:, pl.ds(offset, TILE)], weights, preferred_element_type=jnp.float32
        )

    allowed = (row <= position - first) & (row >= start - first)
    scores = jnp.where(allowed, scores_of(block), masked_score)
    top = jnp.max(scores, axis=0, keepdims=True)
    mixed = mix(scores, top, block)

    def body(at, carry):
        top, mixed = carry
        scores = jnp.where(row >= start - at * TILE, scores_of(at), masked_score)
        higher = jnp.maximum(top, jnp.max(scores, axis=0, keepdims=True))
        fade = jnp.exp2((top - higher) * score_scale)
        return higher, mixed * fade + mix(scores, higher, at)

    top, mixed = lax.fori_loop(low // TILE, block, body, (top, mixed))
    result = (mixed[:HD] / mixed[HD : HD + 1]).T.astype(jnp.bfloat16)
    out[:, :HD] = result[:TILE]
    out[:, HD:] = result[TILE:]


def attend(source, text_at, ends, slots, text, keys, values, base, half, column):
    in_specs = [
        pl.BlockSpec((1, TILE, WIDE), lambda i, s, t, e: (s[i], 0, column)),
        pl.BlockSpec((TILE, WIDE), lambda i, s, t, e: (0, column)),
        pl.BlockSpec((SEQ, HD), lambda i, s, t, e: (0, 0)),
        pl.BlockSpec((HD + TAIL, SEQ), lambda i, s, t, e: (0, 0)),
    ]
    operands = [source, text_at, ends, slots, text, keys, values]
    aliases = {}
    if base is not None:
        in_specs.append(pl.BlockSpec(memory_space=pl.ANY))
        operands.append(base)
        aliases = {7: 0}
    grid_spec = pltpu.PrefetchScalarGridSpec(
        num_scalar_prefetch=3,
        grid=(BLOCKS,),
        in_specs=in_specs,
        out_specs=pl.BlockSpec((TILE, WIDE), lambda i, s, t, e: (i, half)),
    )

    def body(*refs):
        attend_kernel(base is not None, *refs)

    return pl.pallas_call(
        body,
        grid_spec=grid_spec,
        out_shape=jax.ShapeDtypeStruct((SEQ, 2 * WIDE), jnp.bfloat16),
        input_output_aliases=aliases,
        compiler_params=params(),
        cost_estimate=cost(4 * SEQ * SEQ * WIDE, 6 * SEQ * WIDE, SEQ * SEQ),
        name="attend",
    )(*operands)


def local(
    text_rows,
    vis_rows,
    q_weight,
    kv_weight,
    q_bias,
    kv_bias,
    norm_gain,
    tile_dest,
    tile_block,
    doc_lens,
):
    width = norm_gain.shape[0]
    shards = lax.axis_size("dp")
    me = lax.axis_index("dp")
    tensor_at = lax.axis_index("tensor")
    x_at, high = tensor_at // 2, tensor_at % 2
    z_at, low, core = me // 4, me // 2 % 2, me % 2
    blocks = tile_block[0]
    text_block = sum(range(BLOCKS)) - jnp.sum(blocks)

    def squares(rows):
        floats = rows.astype(jnp.float32)
        return jnp.sum(floats * floats, axis=1)

    text_own = lax.dynamic_slice_in_dim(text_rows, text_block * TILE, TILE, 0)
    spread = jnp.concatenate([squares(vis_rows), squares(text_own)]).reshape(BLOCKS, TILE)

    def share(value, bits):
        return jnp.concatenate([value, swap_dp(value, bits)], axis=0)

    def piece(step):
        rows = lax.dynamic_index_in_dim(pieces, (x_at + step) % 4, 0, keepdims=False)
        rows = lax.dynamic_index_in_dim(rows, core, 1, keepdims=False)
        first = lax.dynamic_index_in_dim(rows, high, 0, keepdims=False)
        second = lax.dynamic_index_in_dim(rows, 1 - high, 0, keepdims=False)
        return jnp.concatenate([first, second], axis=0)

    others = [swap_tensor(vis_rows[: 2 * TILE], 1)]
    q_here = mirror_z(q_weight)
    spread = spread + swap_tensor(spread, 2)
    gathered = share(share(tile_block, 2), 1)
    pieces = kv_weight.reshape(4, 2, 2, CORE_PART, WIDE)
    kv_pieces = [piece(step) for step in range(4)]

    q_here, spread, gathered, rows, *kv_pieces = lock(
        (q_here, spread, gathered, vis_rows, *kv_pieces), others
    )
    others.append(swap_tensor(rows[2 * TILE : 4 * TILE], 1))
    q_here = slide_x(q_here)
    spread = spread + swap_tensor(spread, 4)
    kv_third, kv_first = shift_x(kv_pieces[1], 1), shift_x(kv_pieces[3], 3)

    tables = rope_tables(SEQ, HD)
    q_here, spread, gathered, rows, kv_far, kv_first, kv_third, *tables = lock(
        (q_here, spread, gathered, vis_rows, kv_pieces[2], kv_first, kv_third, *tables), others
    )
    q_low = swap_dp(q_here, 2)
    others.append(swap_tensor(rows[4 * TILE : 5 * TILE], 1))
    spread = spread + swap_tensor(spread, 1)
    kv_second = shift_x(kv_far, 2)
    gathered = share(share(gathered, 4), 8)
    last = jnp.concatenate([rows[5 * TILE :], text_own], axis=0)

    own_half = low == high
    q_pair = jnp.concatenate(
        [jnp.where(own_half, q_here, q_low), jnp.where(own_half, q_low, q_here)], axis=0
    )
    q_pair, last, spread, *kv_pieces = lock(
        (q_pair, last, spread, kv_pieces[0], kv_first, kv_second, kv_third), others
    )
    other_last = swap_tensor(last, 1)
    q_pairs = [q_pair[:, :WIDE], q_pair[:, WIDE:]]

    def over_z(pair):
        return [pair] + [shift_z(pair, step) for step in range(1, 4)]

    q_blocks = over_z(q_pairs[0])
    kv_mine = jnp.stack(kv_pieces)
    kv_theirs = swap_dp(kv_mine, 1)

    scale = lax.rsqrt(spread / width + eps).reshape(SEQ, 1)
    gains = norm_gain.reshape(8, 1, PART)
    gain_own = lax.dynamic_index_in_dim(gains, tensor_at, 0, keepdims=False)
    gain_other = lax.dynamic_index_in_dim(gains, tensor_at ^ 1, 0, keepdims=False)
    own = norm_rows(
        jnp.stack([text_block, core]), (vis_rows, text_rows), ((0, 6), (6, 7)), scale, gain_own
    )
    plain = jnp.stack([jnp.int32(0), core])
    other = norm_rows(
        plain, (*others, other_last), ((0, 2), (2, 4), (4, 5), (5, 7)), scale, gain_other
    )

    held = lock((other, own, kv_theirs, q_pairs[1], gathered, *q_blocks), ())
    other, own, kv_theirs, q_late, gathered = held[:5]
    q_mine = jnp.stack(held[5:])
    q_theirs = swap_dp(q_mine, 1)
    order = [0]
    for bits in (2, 1, 4, 8):
        order = order + [entry ^ bits for entry in order]

    owner_ids = jnp.arange(shards, dtype=jnp.int32)
    source_of = jnp.sum(jnp.where(tile_dest == me, owner_ids[:, None], 0), axis=0)
    my_dest = lax.dynamic_slice_in_dim(tile_dest, me, 1, 0)[0]
    sent = (me ^ jnp.array(order, jnp.int32))[:, None] == my_dest[None, :]
    spots = jnp.concatenate([jnp.sum(jnp.where(sent, gathered, 0), axis=0), text_block[None]])
    dest = jnp.concatenate([my_dest, my_dest[-1:]])
    at_block = blocks[None, :] == jnp.arange(BLOCKS, dtype=jnp.int32)[:, None]
    source = jnp.sum(jnp.where(at_block, source_of[None, :], 0), axis=1)
    text_at = text_block[None]
    ends = jnp.cumsum(doc_lens[0])

    weights = [(kv_mine, kv_theirs, 0), (q_mine, q_theirs, 0)]
    token = []

    def parts(chunk, turns):
        at = []
        for turn in turns:
            group = jnp.where(core == 0, (4 - turn) % 4, turn)
            at.append(group if chunk == 0 else (z_at - group) % 4)
        dtypes = [jnp.bfloat16 if turn else jnp.float32 for turn in turns]
        at = jnp.stack(at).astype(jnp.int32)
        outs = parts_of(at, own, other, *weights[chunk], dtypes, token)
        token[:] = outs[:1]
        return list(outs)

    sums = [parts(0, (1,)), parts(1, (1,))]
    (q_late,) = lock((q_late,), sums[1])
    q_blocks = over_z(q_late)
    sums[0] += parts(0, (2, 3, 0))

    arrived, done = {}, []
    for chunk, turn in [(0, 1), (1, 1), (0, 2), (1, 2), (0, 3), (1, 3), (2, 1), (2, 2), (2, 3)]:
        if (chunk, turn) == (1, 2):
            token[:] = [rows]
            sums[1] += parts(1, (2, 3, 0))
            q_mine = jnp.stack(lock(q_blocks, sums[1][3:]))
            weights.append((q_mine, swap_dp(q_mine, 1), 0))
            sums.append(parts(2, (1, 2, 3, 0)))
        if (chunk, turn) == (2, 1):
            (arrived[0],) = lock((arrived[0],), sums[2][:1])
        rows = sums[chunk][turn - 1]
        guards = done[-2:-1]
        if turn > 1:
            rows, got = lock((rows, arrived[chunk]), guards)
            rows = (rows.astype(jnp.float32) + got.astype(jnp.float32)).astype(jnp.bfloat16)
        elif guards:
            (rows,) = lock((rows,), guards)
        arrived[chunk] = ring_x(rows)
        done.append(arrived[chunk])

    biases = [kv_bias.reshape(1, WIDE), q_bias[None, :WIDE], q_bias[None, WIDE:]]
    routed = []
    for chunks, rotated in (((0, 1), (1, 0, 1, 1)), ((2,), (1, 1))):
        slots, text = finish(
            rotated,
            dest,
            spots,
            [sums[chunk][3] for chunk in chunks],
            [arrived[chunk] for chunk in chunks],
            [biases[chunk] for chunk in chunks],
            tables,
            shards,
        )
        filled = lax.all_to_all(slots, "dp", split_axis=0, concat_axis=0, tiled=True)
        routed.append((filled, text))
    pair = gather_pair(source, text_at, *routed[0])
    context = attend(source, text_at, ends, *routed[0], *pair, None, 0, 1)
    return attend(source, text_at, ends, *routed[1], *pair, context, 1, 0)


def solution(mesh):
    in_specs = (
        P("dp", "tensor"),
        P("dp", "tensor"),
        P("dp", "tensor"),
        P(None, None, "tensor"),
        P("tensor"),
        P(None, "tensor"),
        P(),
        P(),
        P("dp", None),
        P("dp", None),
    )
    out_specs = P("dp", "tensor")
    return jax.shard_map(local, mesh=mesh, in_specs=in_specs, out_specs=out_specs, check_vma=False)
```
